512 devices in a mesh: dp: 8 (over x, z_hi), layer: 4 (over y), tensor: 16 (over z_lo, core).
Axes of the slice: x: 4, y: 4, z: 16 (z_hi: 2, z_lo: 8; z = z_hi * 8 + z_lo), core: 2. Of those that a mesh axis runs over, the one named last changes fastest.
Arguments:
- hidden: bfloat16 [4, 1024, 4096], P('layer', 'dp'), may hold values from -120 to 120
- target: bfloat16 [4, 1024, 1024], P('layer', 'dp'), may hold values from -6 to 6
- value_weight: bfloat16 [4, 4096, 1024], P('layer', None, 'dp'), may hold values from -0.09375 to 0.09375
- quant_scale: float32 [4, 1024], P('layer', 'dp'), may hold values from 0.005 to 0.05
- head_rotation: float32 [4, 128, 128], P('layer'), may hold values from -2.5 to 2.5
- rotation: float32 [4096, 4096], P(('dp', 'layer'), 'tensor'), may hold values from -2.5 to 2.5
Outputs:
- new_rotation: float32 [4096, 4096], P(('dp', 'layer'), 'tensor')
- new_head_rotation: float32 [4, 128, 128], P('layer')
The draws below stay inside these ranges and needn't reach their ends.
All inputs are finite; a program needn't handle non-finite values.
Results may differ from the reference program's by a relative error of at most 0.022.
Values may be sent and summed in bfloat16 or wider, within the bound.
No kernel may reach another device: no remote copies, remote signals or barrier semaphores. Data moves between devices by JAX's collectives and lax.ppermute only.
A program may use at most 64 MiB of HBM per device.

```python
import math
import jax
import jax.numpy as jnp
from jax import lax

D = 4096
HEAD = 128
KV_HEADS = 8
ITERS = 2
KVD = 1024
LAYERS = 4
TOKENS = 1024
N_TENSOR = 16


def hadamard(length):
    indices = jnp.arange(length, dtype=jnp.int32)
    parity = jnp.zeros((length, length), jnp.int32)
    for place in range(length.bit_length() - 1):
        bit_values = indices // 2 ** place % 2
        parity = parity + bit_values[:, None] * bit_values[None, :]
    parity = parity % 2
    return (1 - 2 * parity).astype(jnp.float32)


def signed_table(key, length, copies, factors):
    row_key, col_key = jax.random.split(key)
    row_signs = jax.random.rademacher(row_key, (copies, length, 1), dtype=jnp.float32)
    col_signs = jax.random.rademacher(col_key, (copies, 1, length), dtype=jnp.float32)
    return hadamard(length)[None] * row_signs * col_signs * factors


def draw_rotation(key, part):
    key = jax.random.fold_in(key, 11)
    sign_key, noise_key = jax.random.split(key)
    factors = jnp.exp(0.3 * jax.random.truncated_normal(noise_key, -3.0, 3.0, (1, D, D)))
    return signed_table(sign_key, D, 1, factors)[0]


def draw_head_rotation(key, part):
    key = jax.random.fold_in(key, 12)
    sign_key, noise_key = jax.random.split(key)
    factors = jnp.exp(0.3 * jax.random.truncated_normal(noise_key, -3.0, 3.0, (LAYERS, HEAD, HEAD)))
    return signed_table(sign_key, HEAD, LAYERS, factors)


def draw_hidden(key, part):
    key = jax.random.fold_in(key, 13)
    col_key, row_key, noise_key = jax.random.split(key, 3)
    position = jnp.arange(D, dtype=jnp.float32) / D
    col_scale = 0.3 * 10.0 ** (position[None, None, :] + 0.15 * jax.random.truncated_normal(col_key, -3.0, 3.0, (LAYERS, 1, D)))
    row_scale = jnp.exp(jax.random.uniform(row_key, (LAYERS, TOKENS, 1), minval=math.log(0.5), maxval=math.log(2.0)))
    noise_values = jax.random.truncated_normal(noise_key, -4.0, 4.0, (LAYERS, TOKENS, D))
    return (noise_values * col_scale * row_scale).astype(jnp.bfloat16)


def levels(stream_key, extent, cuts, low, top_value):
    loudness, own = 1.0, jax.random.fold_in(stream_key, 6)
    for dim, shards_of in cuts:
        steps = jnp.exp(jax.random.uniform(jax.random.fold_in(own, dim), (shards_of,), jnp.float32, low / len(cuts), top_value / len(cuts)))
        loudness = loudness * jnp.repeat(steps, extent[dim] // shards_of).reshape([-1 if axis == dim else 1 for axis in range(len(extent))])
    return loudness


def scatter_about(stream_key, extent, deviation, reach, shards=(), held_as=jnp.bfloat16):
    values = deviation * jax.random.normal(stream_key, extent, jnp.float32)
    if shards:
        values = values * levels(stream_key, extent, shards, -0.22, 0.18)
    return jnp.clip(values, -reach, reach).astype(held_as)


def setup_inputs(seed: int = 0) -> dict:
    streams_of = jax.random.split(jax.random.key(seed), 7)
    hidden = draw_hidden(jax.random.fold_in(streams_of[6], 71), 0)
    target = scatter_about(streams_of[1], (LAYERS, TOKENS, KVD), 1.0, 6.0, ((0, 4), (1, 8)))
    value_weight = scatter_about(streams_of[2], (LAYERS, D, KVD), D ** -0.5, 0.09375, ((0, 4), (2, 8)))
    quant_scale = jnp.clip(jnp.exp(math.log(0.05) - 2.3025851 * jax.random.uniform(streams_of[3], (LAYERS, KVD), jnp.float32) ** levels(streams_of[3], (LAYERS, KVD), ((0, 4), (1, 8)), -0.2, 0.2)), 0.005, 0.05)
    head_rotation = draw_head_rotation(jax.random.fold_in(streams_of[6], 71), 0)
    rotation = draw_rotation(jax.random.fold_in(streams_of[6], 71), 0)
    return dict(hidden=hidden, target=target, value_weight=value_weight, quant_scale=quant_scale, head_rotation=head_rotation, rotation=rotation)


precise = lax.Precision.HIGHEST

def apply_heads(matrix, head_matrix):
    height = matrix.shape[0]
    width_head = head_matrix.shape[0]
    groups = matrix.shape[1] // width_head
    shaped = matrix.reshape(height, groups, width_head)
    turned = jnp.einsum('jhp,pq->jhq', shaped, head_matrix, precision=precise)
    return turned.reshape(height, matrix.shape[1])

def head_update(stored, gradient):
    root_head = math.sqrt(stored.shape[0])
    head_skew = (jnp.dot(gradient, stored.T, precision=precise) - jnp.dot(stored, gradient.T, precision=precise)) / root_head
    head_step = 4.0 / jnp.sqrt(jnp.sum(head_skew * head_skew) + 1e-12)
    head_base = jnp.dot(head_skew, stored, precision=precise)
    iterate = stored - head_step * head_base
    for repeat in range(ITERS - 1):
        iterate = stored - 0.5 * head_step * (head_base + jnp.dot(head_skew, iterate, precision=precise))
    return iterate

def reference(hidden, target, value_weight, quant_scale, head_rotation, rotation):
    root_width = math.sqrt(D)
    rotation_low = rotation.astype(jnp.bfloat16)
    gradient = jnp.zeros((D, D), jnp.float32)
    new_heads = []
    for layer_index in range(LAYERS):
        hidden_rows = hidden[layer_index]
        weights = value_weight[layer_index]
        stored = head_rotation[layer_index]
        head_matrix = stored / math.sqrt(HEAD)
        scales = quant_scale[layer_index][None, :]
        rotated = (jnp.dot(hidden_rows, rotation_low, preferred_element_type=jnp.float32) / root_width).astype(jnp.bfloat16)
        unmixed = jnp.dot(rotation_low.T, weights, preferred_element_type=jnp.float32) / root_width
        mixed = apply_heads(unmixed, head_matrix)
        tangent = jnp.tanh(mixed / scales)
        quantized = (scales * tangent).astype(jnp.bfloat16)
        values = jnp.dot(rotated, quantized, preferred_element_type=jnp.float32)
        value_grad = (2.0 * (values - target[layer_index].astype(jnp.float32)) / TOKENS).astype(jnp.bfloat16)
        rotated_grad = jnp.dot(value_grad, quantized.T, preferred_element_type=jnp.float32).astype(jnp.bfloat16)
        quant_grad = jnp.dot(rotated.T, value_grad, preferred_element_type=jnp.float32)
        mixed_grad = quant_grad * (1.0 - tangent * tangent)
        folded = apply_heads(weights.astype(jnp.float32), head_matrix).astype(jnp.bfloat16)
        gradient = gradient + jnp.dot(hidden_rows.T, rotated_grad, preferred_element_type=jnp.float32)
        gradient = gradient + jnp.dot(folded, mixed_grad.astype(jnp.bfloat16).T, preferred_element_type=jnp.float32)
        head_grad = jnp.einsum('jhp,jhq->pq', unmixed.reshape(D, KV_HEADS, HEAD), mixed_grad.reshape(D, KV_HEADS, HEAD), precision=precise)
        new_heads.append(head_update(stored, head_grad))
    grad_low = gradient.astype(jnp.bfloat16)
    range_width = D // N_TENSOR
    skew = jnp.zeros((D, D), jnp.float32)
    for range_index in range(N_TENSOR):
        grad_cols = grad_low[:, range_index * range_width:(range_index + 1) * range_width]
        rotation_cols = rotation_low[:, range_index * range_width:(range_index + 1) * range_width]
        first_term = jnp.dot(grad_cols, rotation_cols.T, preferred_element_type=jnp.float32)
        second_term = jnp.dot(rotation_cols, grad_cols.T, preferred_element_type=jnp.float32)
        rounded = lax.optimization_barrier(((first_term - second_term) / root_width).astype(jnp.bfloat16))
        skew = skew + rounded.astype(jnp.float32)
    step_size = 16.0 / jnp.sqrt(jnp.sum(skew * skew) + 1e-12)
    skew_low = skew.astype(jnp.bfloat16)
    base_term = jnp.dot(skew_low, rotation_low, preferred_element_type=jnp.float32)
    iterate = rotation - step_size * base_term
    for repeat in range(ITERS - 1):
        iterate = rotation - 0.5 * step_size * (base_term + jnp.dot(skew_low, iterate.astype(jnp.bfloat16), preferred_element_type=jnp.float32))
    return (iterate, jnp.stack(new_heads))
```

```python
import math

import jax
import jax.numpy as jnp
from jax import lax
from jax.sharding import Mesh, PartitionSpec as P

D = 4096
HEAD = 128
SIZES = {"x": 4, "zh": 2, "y": 4, "zl": 8, "c": 2}
ALL = tuple(SIZES)
ROWS = 128
COLS = 256

precise = lax.Precision.HIGHEST
first = (((0,), (0,)), ((), ()))
second = (((1,), (1,)), ((), ()))
plain = (((1,), (0,)), ((), ()))


def mul(a, b, dims=plain, precision=None):
    return lax.dot_general(a, b, dims, precision=precision, preferred_element_type=jnp.float32)


def count(axes):
    return math.prod(SIZES[a] for a in axes)


def exchange(blocks, axes):
    n = count(axes)
    flat = blocks.reshape((n * blocks.shape[1],) + blocks.shape[2:])
    out = lax.all_to_all(flat, axes, split_axis=0, concat_axis=0, tiled=True)
    return out.reshape(blocks.shape)


def gather(block, axes):
    return exchange(jnp.broadcast_to(block[None], (count(axes),) + block.shape), axes)


def swap(block, axis):
    return lax.ppermute(block, axis, [(0, 1), (1, 0)])


def added(blocks):
    return jnp.sum(blocks.astype(jnp.float32), 0)


def split_at(array, axis, index):
    mine = lax.dynamic_index_in_dim(array, index, axis, keepdims=False)
    other = lax.dynamic_index_in_dim(array, 1 - index, axis, keepdims=False)
    return mine, other


def head_update(stored, gradient):
    root_head = math.sqrt(stored.shape[0])
    head_skew = (
        jnp.dot(gradient, stored.T, precision=precise)
        - jnp.dot(stored, gradient.T, precision=precise)
    ) / root_head
    head_step = 4.0 / jnp.sqrt(jnp.sum(head_skew * head_skew) + 1e-12)
    head_base = jnp.dot(head_skew, stored, precision=precise)
    iterate = stored - head_step * head_base
    iterate = stored - 0.5 * head_step * (
        head_base + jnp.dot(head_skew, iterate, precision=precise)
    )
    return iterate


def body(hidden, target, value_weight, quant_scale, head_rotation, rotation):
    root_width = math.sqrt(D)
    zh, core = lax.axis_index("zh"), lax.axis_index("c")
    tensor = lax.axis_index(("zl", "c"))
    plane, line = ("x", "y"), ("zl",)
    low = jnp.bfloat16
    rows = hidden[0]
    weights = value_weight[0]
    stored = head_rotation[0]
    head_matrix = stored / math.sqrt(HEAD)
    scales = quant_scale[0][:, None]

    block_low = rotation.astype(low)
    block_far = swap(block_low, "zh")
    panel_own = gather(block_low, plane).reshape(D // 2, COLS)
    panel_far = gather(block_far, plane).reshape(D // 2, COLS)

    rows_own, rows_far = split_at(rows.reshape(ROWS, 4, 2, D // 8), 2, zh)
    weights_own, weights_far = split_at(weights.reshape(4, 2, D // 8, HEAD), 1, zh)
    folded = mul(head_matrix, weights.astype(jnp.float32), (((0,), (1,)), ((), ())), precise)
    left = jnp.concatenate([rows, folded.astype(low)], 0)
    left_own, left_far = split_at(left.reshape(2 * ROWS, 4, 2, D // 8), 2, zh)
    target_own, target_far = split_at(target[0].reshape(ROWS, 4, 2, HEAD), 2, zh)
    target_here = jnp.concatenate(
        [target_own.reshape(ROWS, 4 * HEAD), target_far.reshape(ROWS, 4 * HEAD)], 1
    )
    target_here = lax.dynamic_slice_in_dim(target_here, tensor * 8, 8, 0)

    unmixed = (
        mul(weights_own.reshape(D // 2, HEAD), panel_own, first)
        + mul(weights_far.reshape(D // 2, HEAD), panel_far, first)
    ) / root_width
    mixed = mul(head_matrix, unmixed, first, precise)
    tangent = jnp.tanh(mixed / scales)
    quantized = (scales * tangent).astype(low)
    quantized_far = swap(quantized, "zh")
    heads_own = gather(quantized, ("x",)).reshape(4 * HEAD, COLS)
    heads_far = gather(quantized_far, ("x",)).reshape(4 * HEAD, COLS)
    rotated = (
        (
            mul(rows_own.reshape(ROWS, D // 2), panel_own)
            + mul(rows_far.reshape(ROWS, D // 2), panel_far)
        )
        / root_width
    ).astype(low)
    heads = jnp.concatenate([heads_own, heads_far], 0)

    part = mul(rotated, heads, second).astype(low)
    values = added(exchange(part.reshape(16, 8, 8 * HEAD), ("zl", "c")))
    value_grad = (2.0 * (values - target_here.astype(jnp.float32)) / 1024).astype(low)
    value_grad = gather(value_grad, ("zl", "c")).reshape(ROWS, 8 * HEAD)

    grad_own, grad_far = value_grad[:, : 4 * HEAD], value_grad[:, 4 * HEAD :]
    quant_far = mul(grad_far, rotated, first).astype(low)
    quant_far = added(exchange(quant_far.reshape(4, HEAD, COLS), ("x",))).astype(low)
    quant_far = swap(quant_far, "zh")
    quant_own = mul(grad_own, rotated, first).astype(low)
    quant_own = added(exchange(quant_own.reshape(4, HEAD, COLS), ("x",)))
    quant_grad = quant_own + quant_far.astype(jnp.float32)
    mixed_grad = quant_grad * (1.0 - tangent * tangent)
    rotated_grad = mul(value_grad, heads).astype(low)

    right = jnp.concatenate([rotated_grad, mixed_grad.astype(low)], 0)
    part_far = mul(left_far.reshape(2 * ROWS, D // 2), right, first).astype(low)
    part_far = added(exchange(part_far.reshape(16, ROWS, COLS), plane)).astype(low)
    part_far = swap(part_far, "zh")
    part_own = mul(left_own.reshape(2 * ROWS, D // 2), right, first).astype(low)
    part_own = added(exchange(part_own.reshape(16, ROWS, COLS), plane))
    gradient = (part_own + part_far.astype(jnp.float32)).astype(low)

    head_part = mul(unmixed, mixed_grad, second, precise)
    head_part = added(exchange(head_part.reshape(16, 8, HEAD), ("zl", "c")))
    head_grad = lax.all_gather(head_part, ("x", "zh", "zl", "c"), axis=0, tiled=False)
    head_grad = jnp.sum(head_grad.reshape(8, HEAD, HEAD), 0)
    new_head = head_update(stored, head_grad)

    panels = jnp.stack(
        [jnp.where(zh == 0, panel_own, panel_far), jnp.where(zh == 0, panel_far, panel_own)]
    ).reshape(2, 4, 2, 2, ROWS, COLS)
    panels = panels.transpose(1, 0, 2, 3, 4, 5).reshape(8, 2, COLS, COLS)
    panel_core, panel_mate = split_at(panels, 1, core)
    panel_core = panel_core.reshape(D // 2, COLS)
    panel_mate = panel_mate.reshape(D // 2, COLS)

    product_mate = (mul(panel_mate, gradient, second) / root_width).astype(low)
    product_mate = swap(product_mate, "c")
    product_core = mul(panel_core, gradient, second) / root_width
    product = (product_core + product_mate.astype(jnp.float32)).astype(low)
    product = added(exchange(product.reshape(8, COLS, ROWS), line))
    odd = lax.axis_index("y") % 2
    halves = product.reshape(2, ROWS, ROWS)
    mirrored = []
    for turn in range(2):
        pairs = [
            (p * 16 + k, (2 * k + (turn ^ (p & 1))) * 16 + p // 2)
            for p in range(32)
            for k in range(16)
        ]
        piece = jnp.where(odd == turn, halves[0], halves[1])
        mirrored.append(lax.ppermute(piece, ALL, pairs))
    mirror = jnp.concatenate(
        [
            jnp.where(odd == 0, mirrored[0], mirrored[1]),
            jnp.where(odd == 0, mirrored[1], mirrored[0]),
        ],
        1,
    )
    skew = product.T - mirror
    skew_low = skew.astype(low)

    skew_core = gather(skew_low, line)
    skew_mate = swap(skew_core, "c")
    wide_core = skew_core.transpose(1, 0, 2)
    wide_mate = skew_mate.transpose(1, 0, 2)
    base = mul(wide_core.reshape(ROWS, D // 2), panel_core) + mul(
        wide_mate.reshape(ROWS, D // 2), panel_mate
    )

    square = jnp.sum(jnp.square(skew_core.astype(jnp.float32))) + jnp.sum(
        jnp.square(skew_mate.astype(jnp.float32))
    )
    high = square.astype(low)
    rest = square - high.astype(jnp.float32)
    middle = rest.astype(low)
    least = (rest - middle.astype(jnp.float32)).astype(low)
    terms = jnp.stack([high, middle, least])[:, None]
    extra = jnp.pad(jnp.broadcast_to(terms, (3, COLS)), ((0, 13), (0, 0)))
    message = jnp.concatenate([base.astype(low), extra], 0)
    message_far = swap(message, "zh")
    all_own = gather(message, plane)
    all_far = gather(message_far, plane)

    wide = jnp.where(
        core == 0,
        jnp.stack([wide_core, wide_mate], 2),
        jnp.stack([wide_mate, wide_core], 2),
    )
    wide_own, wide_far = split_at(wide.reshape(ROWS, 4, 2, D // 8), 2, zh)
    twice = mul(
        wide_own.reshape(ROWS, D // 2), all_own[:, :ROWS].reshape(D // 2, COLS)
    ) + mul(wide_far.reshape(ROWS, D // 2), all_far[:, :ROWS].reshape(D // 2, COLS))
    square_sum = jnp.sum(all_own[:, ROWS : ROWS + 3, 0].astype(jnp.float32)) + jnp.sum(
        all_far[:, ROWS : ROWS + 3, 0].astype(jnp.float32)
    )
    step_size = 16.0 / jnp.sqrt(square_sum + 1e-12)
    iterate = rotation - step_size * base + 0.5 * step_size * step_size * twice
    return (iterate, new_head[None])


def solution(mesh):
    split = Mesh(mesh.devices.reshape(tuple(SIZES.values())), ALL)
    dp, tensor = ("x", "zh"), ("zl", "c")
    in_specs = (
        P("y", dp, None),
        P("y", dp, None),
        P("y", None, dp),
        P("y", dp),
        P("y", None, None),
        P(("x", "zh", "y"), tensor),
    )
    out_specs = (P(("x", "zh", "y"), tensor), P("y", None, None))
    return jax.shard_map(body, mesh=split, in_specs=in_specs, out_specs=out_specs, check_vma=False)
```

```python
import math

import jax
import jax.numpy as jnp
from jax import lax
from jax.sharding import Mesh, PartitionSpec as P

D = 4096
HEAD = 128
SIZES = {"x": 4, "zh": 2, "y": 4, "zq": 4, "z1": 2, "c": 2}
ALL = tuple(SIZES)
ROWS = 128
COLS = 256
HALF = D // 2
LONG = COLS + 40
DP = ("x", "zh")
PLANE = ("x", "y")
TENSOR = ("zq", "z1", "c")

precise = lax.Precision.HIGHEST
first = (((0,), (0,)), ((), ()))
second = (((1,), (1,)), ((), ()))
plain = (((1,), (0,)), ((), ()))


def mul(a, b, dims=plain, precision=None):
    return lax.dot_general(a, b, dims, precision=precision, preferred_element_type=jnp.float32)


def count(axes):
    return math.prod(SIZES[a] for a in axes)


def exchange(blocks, axes):
    n = count(axes)
    flat = blocks.reshape((n * blocks.shape[1],) + blocks.shape[2:])
    out = lax.all_to_all(flat, axes, split_axis=0, concat_axis=0, tiled=True)
    return out.reshape(blocks.shape)


def copies(block, axes):
    return jnp.broadcast_to(block[None], (count(axes),) + block.shape)


def gather(block, axes):
    return exchange(copies(block, axes), axes)


hold = lax.optimization_barrier


def swap(block, axis, bit=1):
    n = SIZES[axis]
    return lax.ppermute(block, axis, [(i, i ^ bit) for i in range(n)])


def added(blocks):
    return jnp.sum(blocks.astype(jnp.float32), 0)


def split_at(array, axis, index):
    zero = lax.index_in_dim(array, 0, axis, keepdims=False)
    one = lax.index_in_dim(array, 1, axis, keepdims=False)
    return jnp.where(index == 0, zero, one), jnp.where(index == 0, one, zero)


def in_order(index, mine, other, axis):
    return jnp.where(
        index == 0, jnp.stack([mine, other], axis), jnp.stack([other, mine], axis)
    )


def terms_of(array, axis=-1):
    high = array.astype(jnp.bfloat16)
    rest = (array - high.astype(jnp.float32)).astype(jnp.bfloat16)
    return jnp.concatenate([high, rest], axis)


def three_terms(array):
    high = array.astype(jnp.bfloat16)
    rest = array - high.astype(jnp.float32)
    middle = rest.astype(jnp.bfloat16)
    least = (rest - middle.astype(jnp.float32)).astype(jnp.bfloat16)
    return jnp.stack([high, middle, least])


def value_of(pair):
    pair = pair.astype(jnp.float32)
    return pair[..., :HEAD] + pair[..., HEAD:]


def head_update(stored, gradient):
    root_head = math.sqrt(stored.shape[0])
    head_skew = (
        jnp.dot(gradient, stored.T, precision=precise)
        - jnp.dot(stored, gradient.T, precision=precise)
    ) / root_head
    head_step = 4.0 / jnp.sqrt(jnp.sum(head_skew * head_skew) + 1e-12)
    head_base = jnp.dot(head_skew, stored, precision=precise)
    iterate = stored - head_step * head_base
    iterate = stored - 0.5 * head_step * (
        head_base + jnp.dot(head_skew, iterate, precision=precise)
    )
    return iterate


def body(hidden, target, value_weight, quant_scale, head_rotation, rotation):
    root_width = math.sqrt(D)
    zh, core, stride = lax.axis_index("zh"), lax.axis_index("c"), lax.axis_index("z1")
    tensor = lax.axis_index(TENSOR)
    low = jnp.bfloat16
    rows = hidden[0]
    weights = value_weight[0]
    stored = head_rotation[0]
    head_matrix = stored / math.sqrt(HEAD)
    scales = quant_scale[0][:, None]

    block_low = rotation.astype(low)
    spread, block_low = hold((copies(block_low, PLANE), block_low))
    block_far = swap(block_low, "zh")
    panel_own = exchange(spread, PLANE)
    spread, panel_own = hold((copies(block_far, PLANE), panel_own))
    panel_own = panel_own.reshape(HALF, COLS)
    panel_far = exchange(spread, PLANE)

    rows_own, rows_far = split_at(rows.reshape(ROWS, 4, 2, D // 8), 2, zh)
    rows_own, rows_far = rows_own.reshape(ROWS, HALF), rows_far.reshape(ROWS, HALF)
    weights_own, weights_far = split_at(weights.reshape(4, 2, D // 8, HEAD), 1, zh)
    weights_own, weights_far = weights_own.reshape(HALF, HEAD), weights_far.reshape(HALF, HEAD)
    panel_far, rows_own, rows_far, weights_own, weights_far = hold(
        (panel_far, rows_own, rows_far, weights_own, weights_far)
    )
    panel_far = panel_far.reshape(HALF, COLS)

    unmixed = (mul(weights_own, panel_own, first) + mul(weights_far, panel_far, first)) / root_width
    tangent = jnp.tanh(mul(head_matrix, unmixed, first, precise) / scales)
    quantized = (scales * tangent).astype(low)
    spread, quantized = hold((copies(quantized, ("x",)), quantized))
    heads_own = exchange(spread, ("x",))
    spread, heads_own = hold((copies(swap(quantized, "zh"), ("x",)), heads_own))
    heads_far = exchange(spread, ("x",))
    heads = in_order(zh, heads_own, heads_far, 1).reshape(8 * HEAD, COLS)
    rotated = ((mul(rows_own, panel_own) + mul(rows_far, panel_far)) / root_width).astype(low)

    turned = (((0,), (1,)), ((), ()))
    left_own, left_far = (
        jnp.concatenate(
            [tokens, mul(head_matrix, head.astype(jnp.float32), turned, precise).astype(low)], 0
        )
        for tokens, head in ((rows_own, weights_own), (rows_far, weights_far))
    )
    target_here = lax.dynamic_slice_in_dim(target[0], tensor * 8, 8, 0)

    part = mul(rotated, heads, second).astype(low)
    part = exchange(part.reshape(16, 8, 8 * HEAD), TENSOR)
    part, left_own, left_far, target_here = hold((part, left_own, left_far, target_here))
    values = added(part)
    value_grad = (2.0 * (values - target_here.astype(jnp.float32)) / 1024).astype(low)
    value_grad = gather(value_grad, TENSOR)

    own_core, own_mate = split_at(panel_own.reshape(4, 2, COLS, COLS), 1, core)
    far_core, far_mate = split_at(panel_far.reshape(4, 2, COLS, COLS), 1, core)
    same = stride == zh
    panel_core = jnp.where(
        same, jnp.stack([own_core, far_core]), jnp.stack([far_core, own_core])
    )
    panel_mate = jnp.where(
        same, jnp.stack([own_mate, far_mate]), jnp.stack([far_mate, own_mate])
    )
    value_grad, panel_core, panel_mate = hold((value_grad, panel_core, panel_mate))
    value_grad = value_grad.reshape(ROWS, 8 * HEAD)
    tail = ((0, 0), (0, 0), (0, LONG - COLS), (0, 0))
    padded_core, padded_mate = jnp.pad(panel_core, tail), jnp.pad(panel_mate, tail)
    panel_core, panel_mate = panel_core.reshape(HALF, COLS), panel_mate.reshape(HALF, COLS)

    quant_part = mul(value_grad, rotated, first).astype(low)
    quant_grad = added(exchange(quant_part.reshape(8, HEAD, COLS), DP))
    mixed_grad = quant_grad * (1.0 - tangent * tangent)
    rotated_grad = mul(value_grad, heads).astype(low)

    head_part = terms_of(mul(unmixed, mixed_grad, second, precise))
    head_own, head_far = split_at(head_part.reshape(2, 64, COLS), 0, zh)

    right = jnp.concatenate([rotated_grad, mixed_grad.astype(low)], 0)

    def spread_out(left, heads):
        part = mul(left, right, first).astype(low).reshape(16, ROWS, COLS)
        return jnp.concatenate([part, heads.reshape(16, 4, COLS)], 1)

    far = exchange(spread_out(left_far, head_far), PLANE)
    far, own = hold((far, spread_out(left_own, head_own)))
    heads = jnp.sum(value_of(far[:, ROWS:]).reshape(4, 4, 4, HEAD), 0).reshape(16, HEAD)
    back = swap(jnp.concatenate([added(far[:, :ROWS]).astype(low), terms_of(heads)], 0), "zh")
    own = exchange(own, PLANE)
    gradient = (added(own[:, :ROWS]) + back[:ROWS].astype(jnp.float32)).astype(low)
    heads = jnp.sum(value_of(own[:, ROWS:]).reshape(4, 4, 4, HEAD), 0).reshape(16, HEAD)
    head_part = heads + value_of(back[ROWS:])

    product_mate = swap((mul(panel_mate, gradient, second) / root_width).astype(low), "c")
    product = mul(panel_core, gradient, second) / root_width + product_mate.astype(jnp.float32)
    near, next_to = product[: HALF // 2], product[HALF // 2 :]
    near = (near + swap(next_to.astype(low), "z1").astype(jnp.float32)).astype(low)
    product = added(exchange(near.reshape(4, COLS, ROWS), ("zq",)))
    odd = lax.axis_index("y") % 2
    pairs = [
        (p * 16 + k, (2 * k + p % 2) * 16 + p // 2) for p in range(32) for k in range(16)
    ]
    mirror = lax.ppermute(product, ALL, pairs)
    mine, other = split_at(mirror.reshape(2, ROWS, ROWS), 0, odd)
    other = swap(other, "y")
    mirror = in_order(odd, mine.T, other.T, 0).reshape(COLS, ROWS)
    skew = product - mirror
    square = jnp.broadcast_to(three_terms(jnp.sum(skew * skew))[:, None], (3, ROWS))

    message = jnp.concatenate(
        [skew.astype(low), terms_of(head_part, 0), jnp.pad(square, ((0, 5), (0, 0)))], 0
    )
    near = gather(message, ("zq",))
    far = swap(near, "z1")
    near_mate, far_mate = swap(near, "c"), swap(far, "c")
    base = 0.0
    for block, panel in (
        (near, padded_core[0]),
        (near_mate, padded_mate[0]),
        (far, padded_core[1]),
        (far_mate, padded_mate[1]),
    ):
        base += mul(block.reshape(4 * LONG, ROWS), panel.reshape(4 * LONG, COLS), first)
    rest = sum(added(block[:, COLS:]) for block in (near, near_mate, far, far_mate))
    head_part = rest[:16] + rest[16:32]
    square = jnp.sum(rest[32:35, 0])

    extra = jnp.pad(jnp.broadcast_to(three_terms(square)[:, None], (3, COLS)), ((0, 5), (0, 0)))
    message = jnp.concatenate([base.astype(low), terms_of(head_part), extra], 0)
    message_far = swap(message, "zh")
    all_own = gather(message, PLANE)
    all_far = gather(message_far, PLANE)

    near = in_order(core, near[:, :COLS], near_mate[:, :COLS], 1)
    far = in_order(core, far[:, :COLS], far_mate[:, :COLS], 1)
    skew_own, skew_far = jnp.where(same, near, far), jnp.where(same, far, near)
    twice = mul(
        skew_own.reshape(HALF, ROWS), all_own[:, :ROWS].reshape(HALF, COLS), first
    ) + mul(skew_far.reshape(HALF, ROWS), all_far[:, :ROWS].reshape(HALF, COLS), first)
    square_sum = jnp.sum(all_own[:, ROWS + 16 : ROWS + 19, 0].astype(jnp.float32)) + jnp.sum(
        all_far[:, ROWS + 16 : ROWS + 19, 0].astype(jnp.float32)
    )
    step_size = 16.0 / jnp.sqrt(square_sum + 1e-12)
    iterate = rotation - step_size * base + 0.5 * step_size * step_size * twice

    layer = lax.axis_index("y")
    heads_own = all_own[:, ROWS : ROWS + 16].reshape(16, 4, 4, COLS)
    heads_far = all_far[:, ROWS : ROWS + 16].reshape(16, 4, 4, COLS)
    heads_own = lax.dynamic_index_in_dim(heads_own, layer, 1, keepdims=False)
    heads_far = lax.dynamic_index_in_dim(heads_far, layer, 1, keepdims=False)
    head_grad = value_of(in_order(zh, heads_own, heads_far, 0)).reshape(HEAD, HEAD)
    return (iterate, head_update(stored, head_grad)[None])


def solution(mesh):
    split = Mesh(mesh.devices.reshape(tuple(SIZES.values())), ALL)
    in_specs = (
        P("y", DP, None),
        P("y", DP, None),
        P("y", None, DP),
        P("y", DP),
        P("y", None, None),
        P(("x", "zh", "y"), TENSOR),
    )
    out_specs = (P(("x", "zh", "y"), TENSOR), P("y", None, None))
    return jax.shard_map(body, mesh=split, in_specs=in_specs, out_specs=out_specs, check_vma=False)
```

```python
import math

import jax
import jax.numpy as jnp
from jax import lax
from jax.sharding import Mesh, PartitionSpec as P

D = 4096
HEAD = 128
SIZES = {"x": 4, "zh": 2, "y": 4, "zq": 4, "z1": 2, "c": 2}
ALL = tuple(SIZES)
ROWS = 128
COLS = 256
HALF = D // 2
LONG = COLS + 40
DP = ("x", "zh")
PLANE = ("x", "y")
TENSOR = ("zq", "z1", "c")

precise = lax.Precision.HIGHEST
first = (((0,), (0,)), ((), ()))
second = (((1,), (1,)), ((), ()))
plain = (((1,), (0,)), ((), ()))


def mul(a, b, dims=plain, precision=None):
    return lax.dot_general(a, b, dims, precision=precision, preferred_element_type=jnp.float32)


def count(axes):
    return math.prod(SIZES[a] for a in axes)


def exchange(blocks, axes):
    n = count(axes)
    flat = blocks.reshape((n * blocks.shape[1],) + blocks.shape[2:])
    out = lax.all_to_all(flat, axes, split_axis=0, concat_axis=0, tiled=True)
    return out.reshape(blocks.shape)


def copies(block, axes):
    return jnp.broadcast_to(block[None], (count(axes),) + block.shape)


def gather(block, axes):
    return exchange(copies(block, axes), axes)


hold = lax.optimization_barrier


def swap(block, axis, bit=1):
    n = SIZES[axis]
    return lax.ppermute(block, axis, [(i, i ^ bit) for i in range(n)])


def added(blocks):
    return jnp.sum(blocks.astype(jnp.float32), 0)


def split_at(array, axis, index):
    zero = lax.index_in_dim(array, 0, axis, keepdims=False)
    one = lax.index_in_dim(array, 1, axis, keepdims=False)
    return jnp.where(index == 0, zero, one), jnp.where(index == 0, one, zero)


def in_order(index, mine, other, axis):
    return jnp.where(
        index == 0, jnp.stack([mine, other], axis), jnp.stack([other, mine], axis)
    )


def terms_of(array, axis=-1):
    high = array.astype(jnp.bfloat16)
    rest = (array - high.astype(jnp.float32)).astype(jnp.bfloat16)
    return jnp.concatenate([high, rest], axis)


def three_terms(array):
    high = array.astype(jnp.bfloat16)
    rest = array - high.astype(jnp.float32)
    middle = rest.astype(jnp.bfloat16)
    least = (rest - middle.astype(jnp.float32)).astype(jnp.bfloat16)
    return jnp.stack([high, middle, least])


def value_of(pair):
    pair = pair.astype(jnp.float32)
    return pair[..., :HEAD] + pair[..., HEAD:]


def head_update(stored, gradient):
    root_head = math.sqrt(stored.shape[0])
    head_skew = (
        jnp.dot(gradient, stored.T, precision=precise)
        - jnp.dot(stored, gradient.T, precision=precise)
    ) / root_head
    head_step = 4.0 / jnp.sqrt(jnp.sum(head_skew * head_skew) + 1e-12)
    head_base = jnp.dot(head_skew, stored, precision=precise)
    iterate = stored - head_step * head_base
    iterate = stored - 0.5 * head_step * (
        head_base + jnp.dot(head_skew, iterate, precision=precise)
    )
    return iterate


def body(hidden, target, value_weight, quant_scale, head_rotation, rotation):
    root_width = math.sqrt(D)
    zh, core, stride = lax.axis_index("zh"), lax.axis_index("c"), lax.axis_index("z1")
    tensor = lax.axis_index(TENSOR)
    low = jnp.bfloat16
    rows = hidden[0]
    weights = value_weight[0]
    stored = head_rotation[0]
    head_matrix = stored / math.sqrt(HEAD)
    scales = quant_scale[0][:, None]

    block_low = rotation.astype(low)
    spread, block_low = hold((copies(block_low, PLANE), block_low))
    block_far = swap(block_low, "zh")
    panel_own = exchange(spread, PLANE)
    spread, panel_own = hold((copies(block_far, PLANE), panel_own))
    panel_own = panel_own.reshape(HALF, COLS)
    panel_far = exchange(spread, PLANE)

    rows_own, rows_far = split_at(rows.reshape(ROWS, 4, 2, D // 8), 2, zh)
    rows_own, rows_far = rows_own.reshape(ROWS, HALF), rows_far.reshape(ROWS, HALF)
    weights_own, weights_far = split_at(weights.reshape(4, 2, D // 8, HEAD), 1, zh)
    weights_own, weights_far = weights_own.reshape(HALF, HEAD), weights_far.reshape(HALF, HEAD)
    target_own, target_far = split_at(target[0].reshape(ROWS, 4, 2, HEAD), 2, zh)
    target_own, target_far = (
        lax.dynamic_slice_in_dim(half.reshape(ROWS, 4 * HEAD), tensor % 8 * 16, 16, 0)
        for half in (target_own, target_far)
    )
    panel_far, rows_own, rows_far, weights_own, weights_far, target_far = hold(
        (panel_far, rows_own, rows_far, weights_own, weights_far, target_far)
    )
    panel_far = panel_far.reshape(HALF, COLS)

    rotated = ((mul(rows_own, panel_own) + mul(rows_far, panel_far)) / root_width).astype(low)
    message = swap(jnp.concatenate([rotated, target_far.reshape(32, COLS)], 0), "zh")
    tokens = jnp.concatenate([rotated, message[:ROWS]], 0)
    target_here = jnp.where(tensor < 8, target_own, message[ROWS:].reshape(16, 4 * HEAD))
    unmixed = (mul(weights_own, panel_own, first) + mul(weights_far, panel_far, first)) / root_width
    tangent = jnp.tanh(mul(head_matrix, unmixed, first, precise) / scales)
    quantized = (scales * tangent).astype(low)
    heads = gather(quantized, ("x",)).reshape(4 * HEAD, COLS)

    turned = (((0,), (1,)), ((), ()))
    left_own, left_far = (
        jnp.concatenate(
            [tokens, mul(head_matrix, head.astype(jnp.float32), turned, precise).astype(low)], 0
        )
        for tokens, head in ((rows_own, weights_own), (rows_far, weights_far))
    )
    part = mul(tokens, heads, second).astype(low)
    part = exchange(part.reshape(16, 16, 4 * HEAD), TENSOR)
    part, left_own, left_far, target_here = hold((part, left_own, left_far, target_here))
    values = added(part)
    value_grad = (2.0 * (values - target_here.astype(jnp.float32)) / 1024).astype(low)
    value_grad = gather(value_grad, TENSOR)

    own_core, own_mate = split_at(panel_own.reshape(4, 2, COLS, COLS), 1, core)
    far_core, far_mate = split_at(panel_far.reshape(4, 2, COLS, COLS), 1, core)
    same = stride == zh
    panel_core = jnp.where(
        same, jnp.stack([own_core, far_core]), jnp.stack([far_core, own_core])
    )
    panel_mate = jnp.where(
        same, jnp.stack([own_mate, far_mate]), jnp.stack([far_mate, own_mate])
    )
    value_grad, panel_core, panel_mate = hold((value_grad, panel_core, panel_mate))
    value_grad = value_grad.reshape(2 * ROWS, 4 * HEAD)
    tail = ((0, 0), (0, 0), (0, LONG - COLS), (0, 0))
    padded_core, padded_mate = jnp.pad(panel_core, tail), jnp.pad(panel_mate, tail)
    panel_core, panel_mate = panel_core.reshape(HALF, COLS), panel_mate.reshape(HALF, COLS)

    quant_grad = mul(value_grad, tokens, first).astype(low)
    quant_grad = added(exchange(quant_grad.reshape(4, HEAD, COLS), ("x",)))
    mixed_grad = quant_grad * (1.0 - tangent * tangent)
    rotated_grad = mul(value_grad, heads)
    other = swap(rotated_grad[ROWS:].astype(low), "zh")
    rotated_grad = (rotated_grad[:ROWS] + other.astype(jnp.float32)).astype(low)

    head_part = terms_of(mul(unmixed, mixed_grad, second, precise))
    head_own, head_far = split_at(head_part.reshape(2, 64, COLS), 0, zh)

    right = jnp.concatenate([rotated_grad, mixed_grad.astype(low)], 0)

    def spread_out(left, heads):
        part = mul(left, right, first).astype(low).reshape(16, ROWS, COLS)
        return jnp.concatenate([part, heads.reshape(16, 4, COLS)], 1)

    far = exchange(spread_out(left_far, head_far), PLANE)
    far, own = hold((far, spread_out(left_own, head_own)))
    heads = jnp.sum(value_of(far[:, ROWS:]).reshape(4, 4, 4, HEAD), 0).reshape(16, HEAD)
    back = swap(jnp.concatenate([added(far[:, :ROWS]).astype(low), terms_of(heads)], 0), "zh")
    own = exchange(own, PLANE)
    gradient = (added(own[:, :ROWS]) + back[:ROWS].astype(jnp.float32)).astype(low)
    heads = jnp.sum(value_of(own[:, ROWS:]).reshape(4, 4, 4, HEAD), 0).reshape(16, HEAD)
    head_part = heads + value_of(back[ROWS:])

    product_mate = swap((mul(panel_mate, gradient, second) / root_width).astype(low), "c")
    product = mul(panel_core, gradient, second) / root_width + product_mate.astype(jnp.float32)
    near, next_to = product[: HALF // 2], product[HALF // 2 :]
    near = (near + swap(next_to.astype(low), "z1").astype(jnp.float32)).astype(low)
    product = added(exchange(near.reshape(4, COLS, ROWS), ("zq",)))
    odd = lax.axis_index("y") % 2
    pairs = [
        (p * 16 + k, (2 * k + p % 2) * 16 + p // 2) for p in range(32) for k in range(16)
    ]
    mirror = lax.ppermute(product, ALL, pairs)
    mine, other = split_at(mirror.reshape(2, ROWS, ROWS), 0, odd)
    other = swap(other, "y")
    mirror = in_order(odd, mine.T, other.T, 0).reshape(COLS, ROWS)
    skew = product - mirror
    square = jnp.broadcast_to(three_terms(jnp.sum(skew * skew))[:, None], (3, ROWS))

    message = jnp.concatenate(
        [skew.astype(low), terms_of(head_part, 0), jnp.pad(square, ((0, 5), (0, 0)))], 0
    )
    near = gather(message, ("zq",))
    far = swap(near, "z1")
    near_mate, far_mate = swap(near, "c"), swap(far, "c")
    base = 0.0
    for block, panel in (
        (near, padded_core[0]),
        (near_mate, padded_mate[0]),
        (far, padded_core[1]),
        (far_mate, padded_mate[1]),
    ):
        base += mul(block.reshape(4 * LONG, ROWS), panel.reshape(4 * LONG, COLS), first)
    rest = sum(added(block[:, COLS:]) for block in (near, near_mate, far, far_mate))
    head_part = rest[:16] + rest[16:32]
    square = jnp.sum(rest[32:35, 0])

    extra = jnp.pad(jnp.broadcast_to(three_terms(square)[:, None], (3, COLS)), ((0, 5), (0, 0)))
    message = jnp.concatenate([base.astype(low), terms_of(head_part), extra], 0)
    message_far = swap(message, "zh")
    all_own = gather(message, PLANE)
    all_far = gather(message_far, PLANE)

    near = in_order(core, near[:, :COLS], near_mate[:, :COLS], 1)
    far = in_order(core, far[:, :COLS], far_mate[:, :COLS], 1)
    skew_own, skew_far = jnp.where(same, near, far), jnp.where(same, far, near)
    twice = mul(
        skew_own.reshape(HALF, ROWS), all_own[:, :ROWS].reshape(HALF, COLS), first
    ) + mul(skew_far.reshape(HALF, ROWS), all_far[:, :ROWS].reshape(HALF, COLS), first)
    square_sum = jnp.sum(all_own[:, ROWS + 16 : ROWS + 19, 0].astype(jnp.float32)) + jnp.sum(
        all_far[:, ROWS + 16 : ROWS + 19, 0].astype(jnp.float32)
    )
    step_size = 16.0 / jnp.sqrt(square_sum + 1e-12)
    iterate = rotation - step_size * base + 0.5 * step_size * step_size * twice

    layer = lax.axis_index("y")
    heads_own = all_own[:, ROWS : ROWS + 16].reshape(16, 4, 4, COLS)
    heads_far = all_far[:, ROWS : ROWS + 16].reshape(16, 4, 4, COLS)
    heads_own = lax.dynamic_index_in_dim(heads_own, layer, 1, keepdims=False)
    heads_far = lax.dynamic_index_in_dim(heads_far, layer, 1, keepdims=False)
    head_grad = value_of(in_order(zh, heads_own, heads_far, 0)).reshape(HEAD, HEAD)
    return (iterate, head_update(stored, head_grad)[None])


def solution(mesh):
    split = Mesh(mesh.devices.reshape(tuple(SIZES.values())), ALL)
    in_specs = (
        P("y", DP, None),
        P("y", DP, None),
        P("y", None, DP),
        P("y", DP),
        P("y", None, None),
        P(("x", "zh", "y"), TENSOR),
    )
    out_specs = (P(("x", "zh", "y"), TENSOR), P("y", None, None))
    return jax.shard_map(body, mesh=split, in_specs=in_specs, out_specs=out_specs, check_vma=False)
```

```python
import math

import jax
import jax.numpy as jnp
from jax import lax
from jax.sharding import Mesh, PartitionSpec as P

D = 4096
HEAD = 128
SIZES = {"x": 4, "zh": 2, "y": 4, "zq": 4, "z1": 2, "c": 2}
ALL = tuple(SIZES)
ROWS = 128
COLS = 256
HALF = D // 2
LONG = COLS + 40
DP = ("x", "zh")
PLANE = ("x", "y")
TENSOR = ("zq", "z1", "c")

precise = lax.Precision.HIGHEST
first = (((0,), (0,)), ((), ()))
second = (((1,), (1,)), ((), ()))
plain = (((1,), (0,)), ((), ()))


def mul(a, b, dims=plain, precision=None):
    return lax.dot_general(a, b, dims, precision=precision, preferred_element_type=jnp.float32)


def count(axes):
    return math.prod(SIZES[a] for a in axes)


def exchange(blocks, axes):
    n = count(axes)
    flat = blocks.reshape((n * blocks.shape[1],) + blocks.shape[2:])
    out = lax.all_to_all(flat, axes, split_axis=0, concat_axis=0, tiled=True)
    return out.reshape(blocks.shape)


def copies(block, axes):
    return jnp.broadcast_to(block[None], (count(axes),) + block.shape)


def gather(block, axes):
    return exchange(copies(block, axes), axes)


hold = lax.optimization_barrier


def swap(block, axis, bit=1):
    n = SIZES[axis]
    return lax.ppermute(block, axis, [(i, i ^ bit) for i in range(n)])


def added(blocks):
    return jnp.sum(blocks.astype(jnp.float32), 0)


def split_at(array, axis, index):
    zero = lax.index_in_dim(array, 0, axis, keepdims=False)
    one = lax.index_in_dim(array, 1, axis, keepdims=False)
    return jnp.where(index == 0, zero, one), jnp.where(index == 0, one, zero)


def in_order(index, mine, other, axis):
    return jnp.where(
        index == 0, jnp.stack([mine, other], axis), jnp.stack([other, mine], axis)
    )


def terms_of(array, axis=-1):
    high = array.astype(jnp.bfloat16)
    rest = (array - high.astype(jnp.float32)).astype(jnp.bfloat16)
    return jnp.concatenate([high, rest], axis)


def three_terms(array):
    high = array.astype(jnp.bfloat16)
    rest = array - high.astype(jnp.float32)
    middle = rest.astype(jnp.bfloat16)
    least = (rest - middle.astype(jnp.float32)).astype(jnp.bfloat16)
    return jnp.stack([high, middle, least])


def value_of(pair):
    pair = pair.astype(jnp.float32)
    return pair[..., :HEAD] + pair[..., HEAD:]


def head_update(stored, gradient):
    root_head = math.sqrt(stored.shape[0])
    head_skew = (
        jnp.dot(gradient, stored.T, precision=precise)
        - jnp.dot(stored, gradient.T, precision=precise)
    ) / root_head
    head_step = 4.0 / jnp.sqrt(jnp.sum(head_skew * head_skew) + 1e-12)
    head_base = jnp.dot(head_skew, stored, precision=precise)
    iterate = stored - head_step * head_base
    iterate = stored - 0.5 * head_step * (
        head_base + jnp.dot(head_skew, iterate, precision=precise)
    )
    return iterate


def body(hidden, target, value_weight, quant_scale, head_rotation, rotation):
    root_width = math.sqrt(D)
    zh, core, stride = lax.axis_index("zh"), lax.axis_index("c"), lax.axis_index("z1")
    tensor = lax.axis_index(TENSOR)
    flip = lax.axis_index("y") // 2 ^ core

    def flipped(blocks):
        column = lax.axis_index("x")
        blocks = jnp.where(column // 2 == 1, jnp.concatenate([blocks[2:], blocks[:2]], 0), blocks)
        turned = jnp.stack([blocks[1], blocks[0], blocks[3], blocks[2]])
        return jnp.where(column % 2 == 1, turned, blocks)

    low = jnp.bfloat16
    rows = hidden[0]
    weights = value_weight[0]
    stored = head_rotation[0]
    head_matrix = stored / math.sqrt(HEAD)
    scales = quant_scale[0][:, None]

    block_low = rotation.astype(low)
    spread, block_low = hold((copies(block_low, PLANE), block_low))
    block_far = swap(block_low, "zh")
    panel_own = exchange(spread, PLANE)
    spread, panel_own = hold((copies(block_far, PLANE), panel_own))
    panel_own = panel_own.reshape(HALF, COLS)
    panel_far = exchange(spread, PLANE)

    rows_own, rows_far = split_at(rows.reshape(ROWS, 4, 2, D // 8), 2, zh)
    rows_own, rows_far = rows_own.reshape(ROWS, HALF), rows_far.reshape(ROWS, HALF)
    weights_own, weights_far = split_at(weights.reshape(4, 2, D // 8, HEAD), 1, zh)
    weights_own, weights_far = weights_own.reshape(HALF, HEAD), weights_far.reshape(HALF, HEAD)
    panel_far, rows_own, rows_far, weights_own, weights_far = hold(
        (panel_far, rows_own, rows_far, weights_own, weights_far)
    )
    panel_far = panel_far.reshape(HALF, COLS)

    rotated = ((mul(rows_own, panel_own) + mul(rows_far, panel_far)) / root_width).astype(low)
    tokens = jnp.concatenate([rotated, swap(rotated, "zh")], 0)
    unmixed = (mul(weights_own, panel_own, first) + mul(weights_far, panel_far, first)) / root_width
    tangent = jnp.tanh(mul(head_matrix, unmixed, first, precise) / scales)
    quantized = (scales * tangent).astype(low)
    heads = gather(quantized, ("x",)).reshape(4 * HEAD, COLS)

    turned = (((0,), (1,)), ((), ()))
    left_own, left_far = (
        jnp.concatenate(
            [tokens, mul(head_matrix, head.astype(jnp.float32), turned, precise).astype(low)], 0
        )
        for tokens, head in ((rows_own, weights_own), (rows_far, weights_far))
    )
    target_own, target_far = split_at(target[0].reshape(ROWS, 4, 2, HEAD), 2, zh)
    target_own, target_far = (
        lax.dynamic_slice_in_dim(half.reshape(ROWS, 4 * HEAD), tensor % 8 * 16, 16, 0)
        for half in (target_own, target_far)
    )
    target_here = jnp.where(tensor < 8, target_own, swap(target_far, "zh"))

    part = mul(tokens, heads, second).astype(low)
    part = exchange(part.reshape(16, 16, 4 * HEAD), TENSOR)
    part, left_own, left_far, target_here = hold((part, left_own, left_far, target_here))
    values = added(part)
    value_grad = (2.0 * (values - target_here.astype(jnp.float32)) / 1024).astype(low)
    value_grad = gather(value_grad, TENSOR)

    own_core, own_mate = split_at(flipped(panel_own.reshape(4, 2, COLS, COLS)), 1, flip)
    far_core, far_mate = split_at(flipped(panel_far.reshape(4, 2, COLS, COLS)), 1, flip)
    same = stride == 0
    panel_core = jnp.where(
        same, jnp.stack([own_core, far_core]), jnp.stack([far_core, own_core])
    )
    panel_mate = jnp.where(
        same, jnp.stack([own_mate, far_mate]), jnp.stack([far_mate, own_mate])
    )
    value_grad, panel_core, panel_mate = hold((value_grad, panel_core, panel_mate))
    value_grad = value_grad.reshape(2 * ROWS, 4 * HEAD)
    tail = ((0, 0), (0, 0), (0, LONG - COLS), (0, 0))
    padded_core, padded_mate = jnp.pad(panel_core, tail), jnp.pad(panel_mate, tail)
    panel_core, panel_mate = panel_core.reshape(HALF, COLS), panel_mate.reshape(HALF, COLS)

    quant_grad = mul(value_grad, tokens, first).astype(low)
    quant_grad = added(exchange(quant_grad.reshape(4, HEAD, COLS), ("x",)))
    mixed_grad = quant_grad * (1.0 - tangent * tangent)
    rotated_grad = mul(value_grad, heads)
    other = swap(rotated_grad[ROWS:].astype(low), "zh")
    rotated_grad = (rotated_grad[:ROWS] + other.astype(jnp.float32)).astype(low)

    head_part = terms_of(mul(unmixed, mixed_grad, second, precise))
    head_own, head_far = split_at(head_part.reshape(2, 64, COLS), 0, zh)

    right = jnp.concatenate([rotated_grad, mixed_grad.astype(low)], 0)

    def spread_out(left, heads):
        part = mul(left, right, first).astype(low).reshape(16, ROWS, COLS)
        return jnp.concatenate([part, heads.reshape(16, 4, COLS)], 1)

    far = exchange(spread_out(left_far, head_far), PLANE)
    far, own = hold((far, spread_out(left_own, head_own)))
    heads = jnp.sum(value_of(far[:, ROWS:]).reshape(4, 4, 4, HEAD), 0).reshape(16, HEAD)
    back = swap(jnp.concatenate([added(far[:, :ROWS]).astype(low), terms_of(heads)], 0), "zh")
    own = exchange(own, PLANE)
    gradient = (added(own[:, :ROWS]) + back[:ROWS].astype(jnp.float32)).astype(low)
    heads = jnp.sum(value_of(own[:, ROWS:]).reshape(4, 4, 4, HEAD), 0).reshape(16, HEAD)
    head_part = heads + value_of(back[ROWS:])

    product_mate = swap((mul(panel_mate, gradient, second) / root_width).astype(low), "c")
    product = mul(panel_core, gradient, second) / root_width + product_mate.astype(jnp.float32)
    near, next_to = product[: HALF // 2], product[HALF // 2 :]
    near = (near + swap(next_to.astype(low), "z1").astype(jnp.float32)).astype(low)
    product = added(exchange(near.reshape(4, COLS, ROWS), ("zq",)))
    odd = lax.axis_index("y") % 2
    pairs = []
    for here in range(512):
        i, h, j, q, o, e = here >> 7, here >> 6 & 1, here >> 4 & 3, here >> 2 & 3, here >> 1 & 1, here & 1
        pairs.append((here, (i ^ q) << 7 | (h ^ o) << 6 | (j ^ 2 * e) << 4 | (here & 15)))
    mirror = lax.ppermute(product.astype(low), ALL, pairs)
    mine, other = split_at(mirror.reshape(2, ROWS, ROWS), 0, odd)
    other = swap(other, "y")
    mirror = in_order(odd, mine.T, other.T, 0).reshape(COLS, ROWS)
    skew = product - mirror.astype(jnp.float32)
    square = jnp.broadcast_to(three_terms(jnp.sum(skew * skew))[:, None], (3, ROWS))

    message = jnp.concatenate(
        [skew.astype(low), terms_of(head_part, 0), jnp.pad(square, ((0, 5), (0, 0)))], 0
    )
    near = gather(message, ("zq",))
    far = swap(near, "z1")
    near_mate, far_mate = swap(near, "c"), swap(far, "c")
    base = 0.0
    for block, panel in (
        (near, padded_core[0]),
        (near_mate, padded_mate[0]),
        (far, padded_core[1]),
        (far_mate, padded_mate[1]),
    ):
        base += mul(block.reshape(4 * LONG, ROWS), panel.reshape(4 * LONG, COLS), first)
    rest = sum(added(block[:, COLS:]) for block in (near, near_mate, far, far_mate))
    head_part = rest[:16] + rest[16:32]
    square = jnp.sum(rest[32:35, 0])

    extra = jnp.pad(jnp.broadcast_to(three_terms(square)[:, None], (3, COLS)), ((0, 5), (0, 0)))
    message = jnp.concatenate([base.astype(low), terms_of(head_part), extra], 0)
    message_far = swap(message, "zh")
    all_own = gather(message, PLANE)
    all_far = gather(message_far, PLANE)

    near = flipped(in_order(flip, near[:, :COLS], near_mate[:, :COLS], 1))
    far = flipped(in_order(flip, far[:, :COLS], far_mate[:, :COLS], 1))
    skew_own, skew_far = jnp.where(same, near, far), jnp.where(same, far, near)
    twice = mul(
        skew_own.reshape(HALF, ROWS), all_own[:, :ROWS].reshape(HALF, COLS), first
    ) + mul(skew_far.reshape(HALF, ROWS), all_far[:, :ROWS].reshape(HALF, COLS), first)
    square_sum = jnp.sum(all_own[:, ROWS + 16 : ROWS + 19, 0].astype(jnp.float32)) + jnp.sum(
        all_far[:, ROWS + 16 : ROWS + 19, 0].astype(jnp.float32)
    )
    step_size = 16.0 / jnp.sqrt(square_sum + 1e-12)
    iterate = rotation - step_size * base + 0.5 * step_size * step_size * twice

    layer = lax.axis_index("y")
    heads_own = all_own[:, ROWS : ROWS + 16].reshape(16, 4, 4, COLS)
    heads_far = all_far[:, ROWS : ROWS + 16].reshape(16, 4, 4, COLS)
    heads_own = lax.dynamic_index_in_dim(heads_own, layer, 1, keepdims=False)
    heads_far = lax.dynamic_index_in_dim(heads_far, layer, 1, keepdims=False)
    head_grad = value_of(in_order(zh, heads_own, heads_far, 0)).reshape(HEAD, HEAD)
    return (iterate, head_update(stored, head_grad)[None])


def solution(mesh):
    split = Mesh(mesh.devices.reshape(tuple(SIZES.values())), ALL)
    in_specs = (
        P("y", DP, None),
        P("y", DP, None),
        P("y", None, DP),
        P("y", DP),
        P("y", None, None),
        P(("x", "zh", "y"), TENSOR),
    )
    out_specs = (P(("x", "zh", "y"), TENSOR), P("y", None, None))
    return jax.shard_map(body, mesh=split, in_specs=in_specs, out_specs=out_specs, check_vma=False)
```

```python
import math

import jax
import jax.numpy as jnp
from jax import lax
from jax.sharding import Mesh, PartitionSpec as P

D = 4096
HEAD = 128
SIZES = {"x": 4, "zh": 2, "y": 4, "zq": 4, "z1": 2, "c": 2}
ALL = tuple(SIZES)
ROWS = 128
COLS = 256
HALF = D // 2
LONG = COLS + 40
DP = ("x", "zh")
PLANE = ("x", "y")
TENSOR = ("zq", "z1", "c")

precise = lax.Precision.HIGHEST
first = (((0,), (0,)), ((), ()))
second = (((1,), (1,)), ((), ()))
plain = (((1,), (0,)), ((), ()))


def mul(a, b, dims=plain, precision=None):
    return lax.dot_general(a, b, dims, precision=precision, preferred_element_type=jnp.float32)


def count(axes):
    return math.prod(SIZES[a] for a in axes)


def exchange(blocks, axes):
    n = count(axes)
    flat = blocks.reshape((n * blocks.shape[1],) + blocks.shape[2:])
    out = lax.all_to_all(flat, axes, split_axis=0, concat_axis=0, tiled=True)
    return out.reshape(blocks.shape)


def copies(block, axes):
    return jnp.broadcast_to(block[None], (count(axes),) + block.shape)


def gather(block, axes):
    return exchange(copies(block, axes), axes)


hold = lax.optimization_barrier


def swap(block, axis, bit=1):
    n = SIZES[axis]
    return lax.ppermute(block, axis, [(i, i ^ bit) for i in range(n)])


def added(blocks):
    return jnp.sum(blocks.astype(jnp.float32), 0)


def split_at(array, axis, index):
    zero = lax.index_in_dim(array, 0, axis, keepdims=False)
    one = lax.index_in_dim(array, 1, axis, keepdims=False)
    return jnp.where(index == 0, zero, one), jnp.where(index == 0, one, zero)


def in_order(index, mine, other, axis):
    return jnp.where(
        index == 0, jnp.stack([mine, other], axis), jnp.stack([other, mine], axis)
    )


def terms_of(array, axis=-1):
    high = array.astype(jnp.bfloat16)
    rest = (array - high.astype(jnp.float32)).astype(jnp.bfloat16)
    return jnp.concatenate([high, rest], axis)


def three_terms(array):
    high = array.astype(jnp.bfloat16)
    rest = array - high.astype(jnp.float32)
    middle = rest.astype(jnp.bfloat16)
    least = (rest - middle.astype(jnp.float32)).astype(jnp.bfloat16)
    return jnp.stack([high, middle, least])


def value_of(pair):
    pair = pair.astype(jnp.float32)
    return pair[..., :HEAD] + pair[..., HEAD:]


def head_update(stored, gradient):
    root_head = math.sqrt(stored.shape[0])
    head_skew = (
        jnp.dot(gradient, stored.T, precision=precise)
        - jnp.dot(stored, gradient.T, precision=precise)
    ) / root_head
    head_step = 4.0 / jnp.sqrt(jnp.sum(head_skew * head_skew) + 1e-12)
    head_base = jnp.dot(head_skew, stored, precision=precise)
    iterate = stored - head_step * head_base
    iterate = stored - 0.5 * head_step * (
        head_base + jnp.dot(head_skew, iterate, precision=precise)
    )
    return iterate


def body(hidden, target, value_weight, quant_scale, head_rotation, rotation):
    root_width = math.sqrt(D)
    zh, core, stride = lax.axis_index("zh"), lax.axis_index("c"), lax.axis_index("z1")
    tensor = lax.axis_index(TENSOR)
    flip = lax.axis_index("y") // 2 ^ core

    def flipped(blocks):
        column = lax.axis_index("x")
        blocks = jnp.where(column // 2 == 1, jnp.concatenate([blocks[2:], blocks[:2]], 0), blocks)
        turned = jnp.stack([blocks[1], blocks[0], blocks[3], blocks[2]])
        return jnp.where(column % 2 == 1, turned, blocks)

    low = jnp.bfloat16
    rows = hidden[0]
    weights = value_weight[0]
    stored = head_rotation[0]
    head_matrix = stored / math.sqrt(HEAD)
    scales = quant_scale[0][:, None]

    block_low = rotation.astype(low)
    spread, block_low = hold((copies(block_low, PLANE), block_low))
    block_far = swap(block_low, "zh")
    panel_own = exchange(spread, PLANE)
    spread, panel_own = hold((copies(block_far, PLANE), panel_own))
    panel_own = panel_own.reshape(HALF, COLS)
    panel_far = exchange(spread, PLANE)

    rows_own, rows_far = split_at(rows.reshape(ROWS, 4, 2, D // 8), 2, zh)
    rows_own, rows_far = rows_own.reshape(ROWS, HALF), rows_far.reshape(ROWS, HALF)
    weights_own, weights_far = split_at(weights.reshape(4, 2, D // 8, HEAD), 1, zh)
    weights_own, weights_far = weights_own.reshape(HALF, HEAD), weights_far.reshape(HALF, HEAD)
    target_own, target_far = split_at(target[0].reshape(ROWS, 4, 2, HEAD), 2, zh)
    target_own, target_far = (
        lax.dynamic_slice_in_dim(half.reshape(ROWS, 4 * HEAD), tensor % 8 * 16, 16, 0)
        for half in (target_own, target_far)
    )
    panel_far, rows_own, rows_far, weights_own, weights_far, target_far = hold(
        (panel_far, rows_own, rows_far, weights_own, weights_far, target_far)
    )
    panel_far = panel_far.reshape(HALF, COLS)

    rotated = ((mul(rows_own, panel_own) + mul(rows_far, panel_far)) / root_width).astype(low)
    message = jnp.concatenate([rotated, target_far.reshape(32, COLS)], 0)
    message, weights_own, weights_far = hold((message, weights_own, weights_far))
    message = swap(message, "zh")
    tokens = jnp.concatenate([rotated, message[:ROWS]], 0)
    target_here = jnp.where(tensor < 8, target_own, message[ROWS:].reshape(16, 4 * HEAD))
    unmixed = (mul(weights_own, panel_own, first) + mul(weights_far, panel_far, first)) / root_width
    tangent = jnp.tanh(mul(head_matrix, unmixed, first, precise) / scales)
    quantized = (scales * tangent).astype(low)
    heads = gather(quantized, ("x",)).reshape(4 * HEAD, COLS)

    turned = (((0,), (1,)), ((), ()))
    left_own, left_far = (
        jnp.concatenate(
            [tokens, mul(head_matrix, head.astype(jnp.float32), turned, precise).astype(low)], 0
        )
        for tokens, head in ((rows_own, weights_own), (rows_far, weights_far))
    )
    part = mul(tokens, heads, second).astype(low)
    part = exchange(part.reshape(16, 16, 4 * HEAD), TENSOR)
    part, left_own, left_far, target_here = hold((part, left_own, left_far, target_here))
    values = added(part)
    value_grad = (2.0 * (values - target_here.astype(jnp.float32)) / 1024).astype(low)
    value_grad = gather(value_grad, TENSOR)

    own_core, own_mate = split_at(flipped(panel_own.reshape(4, 2, COLS, COLS)), 1, flip)
    far_core, far_mate = split_at(flipped(panel_far.reshape(4, 2, COLS, COLS)), 1, flip)
    same = stride == 0
    panel_core = jnp.where(
        same, jnp.stack([own_core, far_core]), jnp.stack([far_core, own_core])
    )
    panel_mate = jnp.where(
        same, jnp.stack([own_mate, far_mate]), jnp.stack([far_mate, own_mate])
    )
    value_grad, panel_core, panel_mate = hold((value_grad, panel_core, panel_mate))
    value_grad = value_grad.reshape(2 * ROWS, 4 * HEAD)
    tail = ((0, 0), (0, 0), (0, LONG - COLS), (0, 0))
    padded_core, padded_mate = jnp.pad(panel_core, tail), jnp.pad(panel_mate, tail)
    panel_core, panel_mate = panel_core.reshape(HALF, COLS), panel_mate.reshape(HALF, COLS)

    quant_grad = mul(value_grad, tokens, first).astype(low)
    quant_grad = added(exchange(quant_grad.reshape(4, HEAD, COLS), ("x",)))
    mixed_grad = quant_grad * (1.0 - tangent * tangent)
    rotated_grad = mul(value_grad, heads)
    other = swap(rotated_grad[ROWS:].astype(low), "zh")
    rotated_grad = (rotated_grad[:ROWS] + other.astype(jnp.float32)).astype(low)

    head_part = terms_of(mul(unmixed, mixed_grad, second, precise))
    head_own, head_far = split_at(head_part.reshape(2, 64, COLS), 0, zh)

    right = jnp.concatenate([rotated_grad, mixed_grad.astype(low)], 0)

    def spread_out(left, heads):
        part = mul(left, right, first).astype(low).reshape(16, ROWS, COLS)
        return jnp.concatenate([part, heads.reshape(16, 4, COLS)], 1)

    far = exchange(spread_out(left_far, head_far), PLANE)
    far, own = hold((far, spread_out(left_own, head_own)))
    heads = jnp.sum(value_of(far[:, ROWS:]).reshape(4, 4, 4, HEAD), 0).reshape(16, HEAD)
    back = swap(jnp.concatenate([added(far[:, :ROWS]).astype(low), terms_of(heads)], 0), "zh")
    own = exchange(own, PLANE)
    gradient = (added(own[:, :ROWS]) + back[:ROWS].astype(jnp.float32)).astype(low)
    heads = jnp.sum(value_of(own[:, ROWS:]).reshape(4, 4, 4, HEAD), 0).reshape(16, HEAD)
    head_part = heads + value_of(back[ROWS:])

    product_mate = swap((mul(panel_mate, gradient, second) / root_width).astype(low), "c")
    product = mul(panel_core, gradient, second) / root_width + product_mate.astype(jnp.float32)
    near, next_to = product[: HALF // 2], product[HALF // 2 :]
    near = (near + swap(next_to.astype(low), "z1").astype(jnp.float32)).astype(low)
    product = added(exchange(near.reshape(4, COLS, ROWS), ("zq",)))
    odd = lax.axis_index("y") % 2
    pairs = []
    for here in range(512):
        i, h, j, q, o, e = here >> 7, here >> 6 & 1, here >> 4 & 3, here >> 2 & 3, here >> 1 & 1, here & 1
        pairs.append((here, (i ^ q) << 7 | (h ^ o) << 6 | (j ^ 2 * e) << 4 | (here & 15)))
    mirror = lax.ppermute(product.astype(low), ALL, pairs)
    mine, other = split_at(mirror.reshape(2, ROWS, ROWS), 0, odd)
    other = swap(other, "y")
    mirror = in_order(odd, mine.T, other.T, 0).reshape(COLS, ROWS)
    skew = product - mirror.astype(jnp.float32)
    square = jnp.broadcast_to(three_terms(jnp.sum(skew * skew))[:, None], (3, ROWS))

    message = jnp.concatenate(
        [skew.astype(low), terms_of(head_part, 0), jnp.pad(square, ((0, 5), (0, 0)))], 0
    )
    near = gather(message, ("zq",))
    far = swap(near, "z1")
    near_mate, far_mate = swap(near, "c"), swap(far, "c")
    base = 0.0
    for block, panel in (
        (near, padded_core[0]),
        (near_mate, padded_mate[0]),
        (far, padded_core[1]),
        (far_mate, padded_mate[1]),
    ):
        base += mul(block.reshape(4 * LONG, ROWS), panel.reshape(4 * LONG, COLS), first)
    rest = sum(added(block[:, COLS:]) for block in (near, near_mate, far, far_mate))
    head_part = rest[:16] + rest[16:32]
    square = jnp.sum(rest[32:35, 0])

    extra = jnp.pad(jnp.broadcast_to(three_terms(square)[:, None], (3, COLS)), ((0, 5), (0, 0)))
    message = jnp.concatenate([base.astype(low), terms_of(head_part), extra], 0)
    message_far = swap(message, "zh")
    all_own = gather(message, PLANE)
    all_far = gather(message_far, PLANE)

    near = flipped(in_order(flip, near[:, :COLS], near_mate[:, :COLS], 1))
    far = flipped(in_order(flip, far[:, :COLS], far_mate[:, :COLS], 1))
    skew_own, skew_far = jnp.where(same, near, far), jnp.where(same, far, near)
    twice = mul(
        skew_own.reshape(HALF, ROWS), all_own[:, :ROWS].reshape(HALF, COLS), first
    ) + mul(skew_far.reshape(HALF, ROWS), all_far[:, :ROWS].reshape(HALF, COLS), first)
    square_sum = jnp.sum(all_own[:, ROWS + 16 : ROWS + 19, 0].astype(jnp.float32)) + jnp.sum(
        all_far[:, ROWS + 16 : ROWS + 19, 0].astype(jnp.float32)
    )
    step_size = 16.0 / jnp.sqrt(square_sum + 1e-12)
    iterate = rotation - step_size * base + 0.5 * step_size * step_size * twice

    layer = lax.axis_index("y")
    heads_own = all_own[:, ROWS : ROWS + 16].reshape(16, 4, 4, COLS)
    heads_far = all_far[:, ROWS : ROWS + 16].reshape(16, 4, 4, COLS)
    heads_own = lax.dynamic_index_in_dim(heads_own, layer, 1, keepdims=False)
    heads_far = lax.dynamic_index_in_dim(heads_far, layer, 1, keepdims=False)
    head_grad = value_of(in_order(zh, heads_own, heads_far, 0)).reshape(HEAD, HEAD)
    return (iterate, head_update(stored, head_grad)[None])


def solution(mesh):
    split = Mesh(mesh.devices.reshape(tuple(SIZES.values())), ALL)
    in_specs = (
        P("y", DP, None),
        P("y", DP, None),
        P("y", None, DP),
        P("y", DP),
        P("y", None, None),
        P(("x", "zh", "y"), TENSOR),
    )
    out_specs = (P(("x", "zh", "y"), TENSOR), P("y", None, None))
    return jax.shard_map(body, mesh=split, in_specs=in_specs, out_specs=out_specs, check_vma=False)
```

```python
import math

import jax
import jax.numpy as jnp
from jax import lax
from jax.sharding import Mesh, PartitionSpec as P

D = 4096
HEAD = 128
SIZES = {"x": 4, "zh": 2, "y": 4, "zq": 4, "z1": 2, "c": 2}
ALL = tuple(SIZES)
ROWS = 128
COLS = 256
HALF = D // 2
LONG = COLS + 40
DP = ("x", "zh")
PLANE = ("x", "y")
TENSOR = ("zq", "z1", "c")

precise = lax.Precision.HIGHEST
first = (((0,), (0,)), ((), ()))
second = (((1,), (1,)), ((), ()))
plain = (((1,), (0,)), ((), ()))


def mul(a, b, dims=plain, precision=None):
    return lax.dot_general(a, b, dims, precision=precision, preferred_element_type=jnp.float32)


def count(axes):
    return math.prod(SIZES[a] for a in axes)


def exchange(blocks, axes):
    n = count(axes)
    flat = blocks.reshape((n * blocks.shape[1],) + blocks.shape[2:])
    out = lax.all_to_all(flat, axes, split_axis=0, concat_axis=0, tiled=True)
    return out.reshape(blocks.shape)


def copies(block, axes):
    return jnp.broadcast_to(block[None], (count(axes),) + block.shape)


def gather(block, axes):
    return exchange(copies(block, axes), axes)


hold = lax.optimization_barrier


def swap(block, axis, bit=1):
    n = SIZES[axis]
    return lax.ppermute(block, axis, [(i, i ^ bit) for i in range(n)])


def added(blocks):
    return jnp.sum(blocks.astype(jnp.float32), 0)


def split_at(array, axis, index):
    zero = lax.index_in_dim(array, 0, axis, keepdims=False)
    one = lax.index_in_dim(array, 1, axis, keepdims=False)
    return jnp.where(index == 0, zero, one), jnp.where(index == 0, one, zero)


def in_order(index, mine, other, axis):
    return jnp.where(
        index == 0, jnp.stack([mine, other], axis), jnp.stack([other, mine], axis)
    )


def terms_of(array, axis=-1):
    high = array.astype(jnp.bfloat16)
    rest = (array - high.astype(jnp.float32)).astype(jnp.bfloat16)
    return jnp.concatenate([high, rest], axis)


def three_terms(array):
    high = array.astype(jnp.bfloat16)
    rest = array - high.astype(jnp.float32)
    middle = rest.astype(jnp.bfloat16)
    least = (rest - middle.astype(jnp.float32)).astype(jnp.bfloat16)
    return jnp.stack([high, middle, least])


def value_of(pair):
    pair = pair.astype(jnp.float32)
    return pair[..., :HEAD] + pair[..., HEAD:]


def head_update(stored, gradient):
    root_head = math.sqrt(stored.shape[0])
    head_skew = (
        jnp.dot(gradient, stored.T, precision=precise)
        - jnp.dot(stored, gradient.T, precision=precise)
    ) / root_head
    head_step = 4.0 / jnp.sqrt(jnp.sum(head_skew * head_skew) + 1e-12)
    head_base = jnp.dot(head_skew, stored, precision=precise)
    iterate = stored - head_step * head_base
    iterate = stored - 0.5 * head_step * (
        head_base + jnp.dot(head_skew, iterate, precision=precise)
    )
    return iterate


def body(hidden, target, value_weight, quant_scale, head_rotation, rotation):
    root_width = math.sqrt(D)
    zh, core, stride = lax.axis_index("zh"), lax.axis_index("c"), lax.axis_index("z1")
    tensor = lax.axis_index(TENSOR)
    flip = lax.axis_index("y") // 2 ^ core

    def flipped(blocks):
        column = lax.axis_index("x")
        blocks = jnp.where(column // 2 == 1, jnp.concatenate([blocks[2:], blocks[:2]], 0), blocks)
        turned = jnp.stack([blocks[1], blocks[0], blocks[3], blocks[2]])
        return jnp.where(column % 2 == 1, turned, blocks)

    low = jnp.bfloat16
    rows = hidden[0]
    weights = value_weight[0]
    stored = head_rotation[0]
    head_matrix = stored / math.sqrt(HEAD)
    scales = quant_scale[0][:, None]

    block_low = rotation.astype(low)
    spread, block_low = hold((copies(block_low, PLANE), block_low))
    block_far = swap(block_low, "zh")
    panel_own = exchange(spread, PLANE)
    spread, panel_own = hold((copies(block_far, PLANE), panel_own))
    panel_own = panel_own.reshape(HALF, COLS)
    panel_far = exchange(spread, PLANE)

    rows_own, rows_far = split_at(rows.reshape(ROWS, 4, 2, D // 8), 2, zh)
    rows_own, rows_far = rows_own.reshape(ROWS, HALF), rows_far.reshape(ROWS, HALF)
    weights_own, weights_far = split_at(weights.reshape(4, 2, D // 8, HEAD), 1, zh)
    weights_own, weights_far = weights_own.reshape(HALF, HEAD), weights_far.reshape(HALF, HEAD)
    target_own, target_far = split_at(target[0].reshape(ROWS, 4, 2, HEAD), 2, zh)
    target_own, target_far = (
        lax.dynamic_slice_in_dim(half.reshape(ROWS, 4 * HEAD), tensor % 8 * 16, 16, 0)
        for half in (target_own, target_far)
    )
    panel_far, rows_own, rows_far, weights_own, weights_far, target_far = hold(
        (panel_far, rows_own, rows_far, weights_own, weights_far, target_far)
    )
    panel_far = panel_far.reshape(HALF, COLS)

    rotated = ((mul(rows_own, panel_own) + mul(rows_far, panel_far)) / root_width).astype(low)
    message = jnp.concatenate([rotated, target_far.reshape(32, COLS)], 0)
    message, weights_own, weights_far = hold((message, weights_own, weights_far))
    message = swap(message, "zh")
    tokens = jnp.concatenate([rotated, message[:ROWS]], 0)
    target_here = jnp.where(tensor < 8, target_own, message[ROWS:].reshape(16, 4 * HEAD))
    unmixed = (mul(weights_own, panel_own, first) + mul(weights_far, panel_far, first)) / root_width
    tangent = jnp.tanh(mul(head_matrix, unmixed, first, precise) / scales)
    quantized = (scales * tangent).astype(low)
    heads = gather(quantized, ("x",)).reshape(4 * HEAD, COLS)

    turned = (((0,), (1,)), ((), ()))
    left_own, left_far = (
        jnp.concatenate(
            [tokens, mul(head_matrix, head.astype(jnp.float32), turned, precise).astype(low)], 0
        )
        for tokens, head in ((rows_own, weights_own), (rows_far, weights_far))
    )
    part_far = mul(message, heads, second)[:ROWS]
    part = jnp.concatenate([mul(rotated, heads, second).astype(low), part_far.astype(low)], 0)
    part = exchange(part.reshape(16, 16, 4 * HEAD), TENSOR)
    part, left_own, left_far, target_here = hold((part, left_own, left_far, target_here))
    values = added(part)
    value_grad = (2.0 * (values - target_here.astype(jnp.float32)) / 1024).astype(low)
    value_grad = gather(value_grad, TENSOR)

    own_core, own_mate = split_at(flipped(panel_own.reshape(4, 2, COLS, COLS)), 1, flip)
    far_core, far_mate = split_at(flipped(panel_far.reshape(4, 2, COLS, COLS)), 1, flip)
    same = stride == 0
    panel_core = jnp.where(
        same, jnp.stack([own_core, far_core]), jnp.stack([far_core, own_core])
    )
    panel_mate = jnp.where(
        same, jnp.stack([own_mate, far_mate]), jnp.stack([far_mate, own_mate])
    )
    value_grad, panel_core, panel_mate = hold((value_grad, panel_core, panel_mate))
    value_grad = value_grad.reshape(2 * ROWS, 4 * HEAD)
    tail = ((0, 0), (0, 0), (0, LONG - COLS), (0, 0))
    padded_core, padded_mate = jnp.pad(panel_core, tail), jnp.pad(panel_mate, tail)
    panel_core, panel_mate = panel_core.reshape(HALF, COLS), panel_mate.reshape(HALF, COLS)

    quant_grad = mul(value_grad, tokens, first).astype(low)
    quant_grad = added(exchange(quant_grad.reshape(4, HEAD, COLS), ("x",)))
    mixed_grad = quant_grad * (1.0 - tangent * tangent)
    rotated_grad = mul(value_grad, heads)
    other = swap(rotated_grad[ROWS:].astype(low), "zh")
    rotated_grad = (rotated_grad[:ROWS] + other.astype(jnp.float32)).astype(low)

    head_part = terms_of(mul(unmixed, mixed_grad, second, precise))
    head_own, head_far = split_at(head_part.reshape(2, 64, COLS), 0, zh)

    right = jnp.concatenate([rotated_grad, mixed_grad.astype(low)], 0)

    def spread_out(left, heads):
        part = mul(left, right, first).astype(low).reshape(16, ROWS, COLS)
        return jnp.concatenate([part, heads.reshape(16, 4, COLS)], 1)

    far = exchange(spread_out(left_far, head_far), PLANE)
    far, own = hold((far, spread_out(left_own, head_own)))
    heads = jnp.sum(value_of(far[:, ROWS:]).reshape(4, 4, 4, HEAD), 0).reshape(16, HEAD)
    back = swap(jnp.concatenate([added(far[:, :ROWS]).astype(low), terms_of(heads)], 0), "zh")
    own = exchange(own, PLANE)
    gradient = (added(own[:, :ROWS]) + back[:ROWS].astype(jnp.float32)).astype(low)
    heads = jnp.sum(value_of(own[:, ROWS:]).reshape(4, 4, 4, HEAD), 0).reshape(16, HEAD)
    head_part = heads + value_of(back[ROWS:])

    product_mate = swap((mul(panel_mate, gradient, second) / root_width).astype(low), "c")
    product = mul(panel_core, gradient, second) / root_width + product_mate.astype(jnp.float32)
    near, next_to = product[: HALF // 2], product[HALF // 2 :]
    near = (near + swap(next_to.astype(low), "z1").astype(jnp.float32)).astype(low)
    product = added(exchange(near.reshape(4, COLS, ROWS), ("zq",)))
    odd = lax.axis_index("y") % 2
    pairs = []
    for here in range(512):
        i, h, j, q, o, e = here >> 7, here >> 6 & 1, here >> 4 & 3, here >> 2 & 3, here >> 1 & 1, here & 1
        pairs.append((here, (i ^ q) << 7 | (h ^ o) << 6 | (j ^ 2 * e) << 4 | (here & 15)))
    mirror = lax.ppermute(product.astype(low), ALL, pairs)
    mine, other = split_at(mirror.reshape(2, ROWS, ROWS), 0, odd)
    other = swap(other, "y")
    mirror = in_order(odd, mine.T, other.T, 0).reshape(COLS, ROWS)
    skew = product - mirror.astype(jnp.float32)
    square = jnp.broadcast_to(three_terms(jnp.sum(skew * skew))[:, None], (3, ROWS))

    message = jnp.concatenate(
        [skew.astype(low), terms_of(head_part, 0), jnp.pad(square, ((0, 5), (0, 0)))], 0
    )
    near = gather(message, ("zq",))
    far = swap(near, "z1")
    near_mate, far_mate = swap(near, "c"), swap(far, "c")
    base = 0.0
    for block, panel in (
        (near, padded_core[0]),
        (near_mate, padded_mate[0]),
        (far, padded_core[1]),
        (far_mate, padded_mate[1]),
    ):
        base += mul(block.reshape(4 * LONG, ROWS), panel.reshape(4 * LONG, COLS), first)
    rest = sum(added(block[:, COLS:]) for block in (near, near_mate, far, far_mate))
    head_part = rest[:16] + rest[16:32]
    square = jnp.sum(rest[32:35, 0])

    extra = jnp.pad(jnp.broadcast_to(three_terms(square)[:, None], (3, COLS)), ((0, 5), (0, 0)))
    message = jnp.concatenate([base.astype(low), terms_of(head_part), extra], 0)
    message_far = swap(message, "zh")
    all_own = gather(message, PLANE)
    all_far = gather(message_far, PLANE)

    near = flipped(in_order(flip, near[:, :COLS], near_mate[:, :COLS], 1))
    far = flipped(in_order(flip, far[:, :COLS], far_mate[:, :COLS], 1))
    skew_own, skew_far = jnp.where(same, near, far), jnp.where(same, far, near)
    twice = mul(
        skew_own.reshape(HALF, ROWS), all_own[:, :ROWS].reshape(HALF, COLS), first
    ) + mul(skew_far.reshape(HALF, ROWS), all_far[:, :ROWS].reshape(HALF, COLS), first)
    square_sum = jnp.sum(all_own[:, ROWS + 16 : ROWS + 19, 0].astype(jnp.float32)) + jnp.sum(
        all_far[:, ROWS + 16 : ROWS + 19, 0].astype(jnp.float32)
    )
    step_size = 16.0 / jnp.sqrt(square_sum + 1e-12)
    iterate = rotation - step_size * base + 0.5 * step_size * step_size * twice

    layer = lax.axis_index("y")
    heads_own = all_own[:, ROWS : ROWS + 16].reshape(16, 4, 4, COLS)
    heads_far = all_far[:, ROWS : ROWS + 16].reshape(16, 4, 4, COLS)
    heads_own = lax.dynamic_index_in_dim(heads_own, layer, 1, keepdims=False)
    heads_far = lax.dynamic_index_in_dim(heads_far, layer, 1, keepdims=False)
    head_grad = value_of(in_order(zh, heads_own, heads_far, 0)).reshape(HEAD, HEAD)
    return (iterate, head_update(stored, head_grad)[None])


def solution(mesh):
    split = Mesh(mesh.devices.reshape(tuple(SIZES.values())), ALL)
    in_specs = (
        P("y", DP, None),
        P("y", DP, None),
        P("y", None, DP),
        P("y", DP),
        P("y", None, None),
        P(("x", "zh", "y"), TENSOR),
    )
    out_specs = (P(("x", "zh", "y"), TENSOR), P("y", None, None))
    return jax.shard_map(body, mesh=split, in_specs=in_specs, out_specs=out_specs, check_vma=False)
```

```python
import math

import jax
import jax.numpy as jnp
from jax import lax
from jax.sharding import Mesh, PartitionSpec as P

D = 4096
HEAD = 128
SIZES = {"x": 4, "zh": 2, "y": 4, "zq": 4, "z1": 2, "c": 2}
ALL = tuple(SIZES)
ROWS = 128
COLS = 256
HALF = D // 2
LONG = COLS + 40
DP = ("x", "zh")
PLANE = ("x", "y")
TENSOR = ("zq", "z1", "c")

precise = lax.Precision.HIGHEST
first = (((0,), (0,)), ((), ()))
second = (((1,), (1,)), ((), ()))
plain = (((1,), (0,)), ((), ()))


def mul(a, b, dims=plain, precision=None):
    return lax.dot_general(a, b, dims, precision=precision, preferred_element_type=jnp.float32)


def count(axes):
    return math.prod(SIZES[a] for a in axes)


def exchange(blocks, axes):
    n = count(axes)
    flat = blocks.reshape((n * blocks.shape[1],) + blocks.shape[2:])
    out = lax.all_to_all(flat, axes, split_axis=0, concat_axis=0, tiled=True)
    return out.reshape(blocks.shape)


def copies(block, axes):
    return jnp.broadcast_to(block[None], (count(axes),) + block.shape)


def gather(block, axes):
    return exchange(copies(block, axes), axes)


hold = lax.optimization_barrier


def swap(block, axis, bit=1):
    n = SIZES[axis]
    return lax.ppermute(block, axis, [(i, i ^ bit) for i in range(n)])


def added(blocks):
    return jnp.sum(blocks.astype(jnp.float32), 0)


def split_at(array, axis, index):
    zero = lax.index_in_dim(array, 0, axis, keepdims=False)
    one = lax.index_in_dim(array, 1, axis, keepdims=False)
    return jnp.where(index == 0, zero, one), jnp.where(index == 0, one, zero)


def in_order(index, mine, other, axis):
    return jnp.where(
        index == 0, jnp.stack([mine, other], axis), jnp.stack([other, mine], axis)
    )


def terms_of(array, axis=-1):
    high = array.astype(jnp.bfloat16)
    rest = (array - high.astype(jnp.float32)).astype(jnp.bfloat16)
    return jnp.concatenate([high, rest], axis)


def three_terms(array):
    high = array.astype(jnp.bfloat16)
    rest = array - high.astype(jnp.float32)
    middle = rest.astype(jnp.bfloat16)
    least = (rest - middle.astype(jnp.float32)).astype(jnp.bfloat16)
    return jnp.stack([high, middle, least])


def value_of(pair):
    pair = pair.astype(jnp.float32)
    return pair[..., :HEAD] + pair[..., HEAD:]


def head_update(stored, gradient):
    root_head = math.sqrt(stored.shape[0])
    head_skew = (
        jnp.dot(gradient, stored.T, precision=precise)
        - jnp.dot(stored, gradient.T, precision=precise)
    ) / root_head
    head_step = 4.0 / jnp.sqrt(jnp.sum(head_skew * head_skew) + 1e-12)
    head_base = jnp.dot(head_skew, stored, precision=precise)
    iterate = stored - head_step * head_base
    iterate = stored - 0.5 * head_step * (
        head_base + jnp.dot(head_skew, iterate, precision=precise)
    )
    return iterate


def body(hidden, target, value_weight, quant_scale, head_rotation, rotation):
    root_width = math.sqrt(D)
    zh, core, stride = lax.axis_index("zh"), lax.axis_index("c"), lax.axis_index("z1")
    tensor = lax.axis_index(TENSOR)
    flip = lax.axis_index("y") // 2 ^ core

    def flipped(blocks):
        column = lax.axis_index("x")
        blocks = jnp.where(column // 2 == 1, jnp.concatenate([blocks[2:], blocks[:2]], 0), blocks)
        turned = jnp.stack([blocks[1], blocks[0], blocks[3], blocks[2]])
        return jnp.where(column % 2 == 1, turned, blocks)

    low = jnp.bfloat16
    rows = hidden[0]
    weights = value_weight[0]
    stored = head_rotation[0]
    head_matrix = stored / math.sqrt(HEAD)
    scales = quant_scale[0][:, None]

    block_low = rotation.astype(low)
    spread, block_low = hold((copies(block_low, PLANE), block_low))
    block_far = swap(block_low, "zh")
    panel_own = exchange(spread, PLANE)
    spread, panel_own = hold((copies(block_far, PLANE), panel_own))
    panel_own = panel_own.reshape(HALF, COLS)
    panel_far = exchange(spread, PLANE)

    rows_own, rows_far = split_at(rows.reshape(ROWS, 4, 2, D // 8), 2, zh)
    rows_own, rows_far = rows_own.reshape(ROWS, HALF), rows_far.reshape(ROWS, HALF)
    weights_own, weights_far = split_at(weights.reshape(4, 2, D // 8, HEAD), 1, zh)
    weights_own, weights_far = weights_own.reshape(HALF, HEAD), weights_far.reshape(HALF, HEAD)
    target_own, target_far = split_at(target[0].reshape(ROWS, 4, 2, HEAD), 2, zh)
    target_own, target_far = (
        lax.dynamic_slice_in_dim(half.reshape(ROWS, 4 * HEAD), tensor % 8 * 16, 16, 0)
        for half in (target_own, target_far)
    )
    panel_far, rows_own, rows_far, weights_own, weights_far, target_far = hold(
        (panel_far, rows_own, rows_far, weights_own, weights_far, target_far)
    )
    panel_far = panel_far.reshape(HALF, COLS)

    rotated = ((mul(rows_own, panel_own) + mul(rows_far, panel_far)) / root_width).astype(low)
    message = jnp.concatenate([rotated, target_far.reshape(32, COLS)], 0)
    message, weights_own, weights_far = hold((message, weights_own, weights_far))
    message = swap(message, "zh")
    tokens = jnp.concatenate([rotated, message[:ROWS]], 0)
    target_here = jnp.where(tensor < 8, target_own, message[ROWS:].reshape(16, 4 * HEAD))
    unmixed = (mul(weights_own, panel_own, first) + mul(weights_far, panel_far, first)) / root_width
    tangent = jnp.tanh(mul(head_matrix, unmixed, first, precise) / scales)
    quantized = (scales * tangent).astype(low)
    heads = gather(quantized, ("x",)).reshape(4 * HEAD, COLS)

    turned = (((0,), (1,)), ((), ()))
    left_own, left_far = (
        jnp.concatenate(
            [tokens, mul(head_matrix, head.astype(jnp.float32), turned, precise).astype(low)], 0
        )
        for tokens, head in ((rows_own, weights_own), (rows_far, weights_far))
    )
    part = mul(tokens, heads, second).astype(low)
    part = exchange(part.reshape(16, 16, 4 * HEAD), TENSOR)
    part, left_own, left_far, target_here = hold((part, left_own, left_far, target_here))
    values = added(part)
    value_grad = (2.0 * (values - target_here.astype(jnp.float32)) / 1024).astype(low)
    value_grad = gather(value_grad, TENSOR)

    own_core, own_mate = split_at(flipped(panel_own.reshape(4, 2, COLS, COLS)), 1, flip)
    far_core, far_mate = split_at(flipped(panel_far.reshape(4, 2, COLS, COLS)), 1, flip)
    same = stride == 0
    panel_core = jnp.where(
        same, jnp.stack([own_core, far_core]), jnp.stack([far_core, own_core])
    )
    panel_mate = jnp.where(
        same, jnp.stack([own_mate, far_mate]), jnp.stack([far_mate, own_mate])
    )
    value_grad, panel_core, panel_mate = hold((value_grad, panel_core, panel_mate))
    value_grad = value_grad.reshape(2 * ROWS, 4 * HEAD)
    tail = ((0, 0), (0, 0), (0, LONG - COLS), (0, 0))
    padded_core, padded_mate = jnp.pad(panel_core, tail), jnp.pad(panel_mate, tail)
    panel_core, panel_mate = panel_core.reshape(HALF, COLS), panel_mate.reshape(HALF, COLS)

    quant_grad = mul(value_grad, tokens, first).astype(low)
    quant_grad, value_grad = hold((quant_grad, value_grad))
    quant_grad = added(exchange(quant_grad.reshape(4, HEAD, COLS), ("x",)))
    mixed_grad = quant_grad * (1.0 - tangent * tangent)
    rotated_grad = mul(value_grad, heads)
    other = swap(rotated_grad[ROWS:].astype(low), "zh")
    rotated_grad = (rotated_grad[:ROWS] + other.astype(jnp.float32)).astype(low)

    head_part = terms_of(mul(unmixed, mixed_grad, second, precise))
    head_own, head_far = split_at(head_part.reshape(2, 64, COLS), 0, zh)

    right = jnp.concatenate([rotated_grad, mixed_grad.astype(low)], 0)

    def spread_out(left, heads):
        part = mul(left, right, first).astype(low).reshape(16, ROWS, COLS)
        return jnp.concatenate([part, heads.reshape(16, 4, COLS)], 1)

    far = exchange(spread_out(left_far, head_far), PLANE)
    far, own = hold((far, spread_out(left_own, head_own)))
    heads = jnp.sum(value_of(far[:, ROWS:]).reshape(4, 4, 4, HEAD), 0).reshape(16, HEAD)
    back = swap(jnp.concatenate([added(far[:, :ROWS]).astype(low), terms_of(heads)], 0), "zh")
    own = exchange(own, PLANE)
    gradient = (added(own[:, :ROWS]) + back[:ROWS].astype(jnp.float32)).astype(low)
    heads = jnp.sum(value_of(own[:, ROWS:]).reshape(4, 4, 4, HEAD), 0).reshape(16, HEAD)
    head_part = heads + value_of(back[ROWS:])

    product_mate = swap((mul(panel_mate, gradient, second) / root_width).astype(low), "c")
    product = mul(panel_core, gradient, second) / root_width + product_mate.astype(jnp.float32)
    near, next_to = product[: HALF // 2], product[HALF // 2 :]
    near = (near + swap(next_to.astype(low), "z1").astype(jnp.float32)).astype(low)
    product = added(exchange(near.reshape(4, COLS, ROWS), ("zq",)))
    odd = lax.axis_index("y") % 2
    pairs = []
    for here in range(512):
        i, h, j, q, o, e = here >> 7, here >> 6 & 1, here >> 4 & 3, here >> 2 & 3, here >> 1 & 1, here & 1
        pairs.append((here, (i ^ q) << 7 | (h ^ o) << 6 | (j ^ 2 * e) << 4 | (here & 15)))
    mirror = lax.ppermute(product.astype(low), ALL, pairs)
    mine, other = split_at(mirror.reshape(2, ROWS, ROWS), 0, odd)
    other = swap(other, "y")
    mirror = in_order(odd, mine.T, other.T, 0).reshape(COLS, ROWS)
    skew = product - mirror.astype(jnp.float32)
    square = jnp.broadcast_to(three_terms(jnp.sum(skew * skew))[:, None], (3, ROWS))

    message = jnp.concatenate(
        [skew.astype(low), terms_of(head_part, 0), jnp.pad(square, ((0, 5), (0, 0)))], 0
    )
    near = gather(message, ("zq",))
    far = swap(near, "z1")
    near_mate, far_mate = swap(near, "c"), swap(far, "c")
    base = 0.0
    for block, panel in (
        (near, padded_core[0]),
        (near_mate, padded_mate[0]),
        (far, padded_core[1]),
        (far_mate, padded_mate[1]),
    ):
        base += mul(block.reshape(4 * LONG, ROWS), panel.reshape(4 * LONG, COLS), first)
    rest = sum(added(block[:, COLS:]) for block in (near, near_mate, far, far_mate))
    head_part = rest[:16] + rest[16:32]
    square = jnp.sum(rest[32:35, 0])

    extra = jnp.pad(jnp.broadcast_to(three_terms(square)[:, None], (3, COLS)), ((0, 5), (0, 0)))
    message = jnp.concatenate([base.astype(low), terms_of(head_part), extra], 0)
    message_far = swap(message, "zh")
    all_own = gather(message, PLANE)
    all_far = gather(message_far, PLANE)

    near = flipped(in_order(flip, near[:, :COLS], near_mate[:, :COLS], 1))
    far = flipped(in_order(flip, far[:, :COLS], far_mate[:, :COLS], 1))
    skew_own, skew_far = jnp.where(same, near, far), jnp.where(same, far, near)
    twice = mul(
        skew_own.reshape(HALF, ROWS), all_own[:, :ROWS].reshape(HALF, COLS), first
    ) + mul(skew_far.reshape(HALF, ROWS), all_far[:, :ROWS].reshape(HALF, COLS), first)
    square_sum = jnp.sum(all_own[:, ROWS + 16 : ROWS + 19, 0].astype(jnp.float32)) + jnp.sum(
        all_far[:, ROWS + 16 : ROWS + 19, 0].astype(jnp.float32)
    )
    step_size = 16.0 / jnp.sqrt(square_sum + 1e-12)
    iterate = rotation - step_size * base + 0.5 * step_size * step_size * twice

    layer = lax.axis_index("y")
    heads_own = all_own[:, ROWS : ROWS + 16].reshape(16, 4, 4, COLS)
    heads_far = all_far[:, ROWS : ROWS + 16].reshape(16, 4, 4, COLS)
    heads_own = lax.dynamic_index_in_dim(heads_own, layer, 1, keepdims=False)
    heads_far = lax.dynamic_index_in_dim(heads_far, layer, 1, keepdims=False)
    head_grad = value_of(in_order(zh, heads_own, heads_far, 0)).reshape(HEAD, HEAD)
    return (iterate, head_update(stored, head_grad)[None])


def solution(mesh):
    split = Mesh(mesh.devices.reshape(tuple(SIZES.values())), ALL)
    in_specs = (
        P("y", DP, None),
        P("y", DP, None),
        P("y", None, DP),
        P("y", DP),
        P("y", None, None),
        P(("x", "zh", "y"), TENSOR),
    )
    out_specs = (P(("x", "zh", "y"), TENSOR), P("y", None, None))
    return jax.shard_map(body, mesh=split, in_specs=in_specs, out_specs=out_specs, check_vma=False)
```
